256 devices in a mesh: inst: 64 (over y, z, core), tp: 4 (over x).
Axes of the slice: x: 4, y: 4, z: 8, core: 2. Of those that a mesh axis runs over, the one named last changes fastest.
Arguments:
- queries: bfloat16 [8192, 8192], P('inst', 'tp'), may hold values from -130 to 130
- new_keys: bfloat16 [8192, 1024], P('inst', 'tp'), may hold values from -6 to 6
- fresh_values: bfloat16 [8192, 1024], P('inst', 'tp'), may hold values from -6 to 6
- lent_page_pool: bfloat16 [1024, 2, 128, 1024], P('inst', None, None, 'tp'), may hold values from -6 to 6
- page_lender: int32 [2048, 1], P(('inst', 'tp')), may hold values from 0 to 63; in each aligned block of 32 rows (0 to 31, 32 to 63, ...) at most 2 rows name the same one
- page_slot: int32 [2048], P(('inst', 'tp')), may hold values from 0 to 15
- starts: int32 [64], P('inst'), may hold values from 1024 to 4096, as said below
Outputs:
- attended: bfloat16 [8192, 8192], P('inst', 'tp')
The draws below stay inside these ranges and needn't reach their ends.
Inputs may be any that keep to these rules, and one draw needn't show every extreme that they name: `page_lender`: among the 32 entries of one request at most 2 name the same lender, and some lender holds exactly 2 pages of some request. Some request starts exactly at 4096.
All inputs are finite; a program needn't handle non-finite values.
Results may differ from the reference program's by a relative error of at most 0.0035.
Values may be sent and summed in bfloat16 or wider, within the bound.
A program may use at most 128 MiB of HBM per device.

```python
import math
import jax
import jax.numpy as jnp
import numpy as np
from jax import lax

QUERY_HEADS = 64
KEY_VALUE_HEADS = 8
HEAD_SIZE = 128
PAGE_TOKENS = 128
REQUEST_TOKENS = 128
CTX_PAGES = 32
SLOTS = 16
CAP = 2
TOTAL_TOKENS = 8192
PAGES = 2048
POOL_SLOTS = 1024
N_INST = 64


def key_base(key):
    return jax.random.truncated_normal(key, -6.0, 6.0, (TOTAL_TOKENS, KEY_VALUE_HEADS * HEAD_SIZE), jnp.float32)


def draw_new_keys(key, part):
    common_offset = key_base(key)
    return common_offset.astype(jnp.bfloat16)


def draw_queries(key, part):
    key = jax.random.fold_in(key, 12)
    values_drawn = 2.0 * jax.random.truncated_normal(key, -6.0, 6.0, (TOTAL_TOKENS, QUERY_HEADS * HEAD_SIZE), jnp.float32)
    return values_drawn.astype(jnp.bfloat16)


def draw_starts(key, part):
    key = jax.random.fold_in(key, 13)
    whole = CTX_PAGES * PAGE_TOKENS
    count = TOTAL_TOKENS // REQUEST_TOKENS
    starts = jax.random.randint(key, (count,), whole // 4, whole + 1)
    chosen = jax.random.randint(jax.random.fold_in(key, 1), (), 0, count)
    return jnp.where(jnp.arange(count) == chosen, whole, starts).astype(jnp.int32)


def set_ends(result, rng, low, high):
    index_at = [jax.random.randint(jax.random.fold_in(rng, axis), (), 0, length) for axis, length in enumerate(result.shape)]
    main_axis = result.shape.index(max(result.shape))
    next_to = index_at[:main_axis] + [(index_at[main_axis] + 1) % result.shape[main_axis]] + index_at[main_axis + 1:]
    return result.at[tuple(index_at)].set(low).at[tuple(next_to)].set(high)


def shard_levels(stream_key, shape, split, low, high):
    factor_of = 1.0
    for dim, parts in split:
        heights = jax.random.uniform(jax.random.fold_in(jax.random.fold_in(stream_key, 6), dim), (parts,), jnp.float32, low / len(split), high / len(split))
        factor_of = factor_of * jnp.repeat(jnp.exp(heights), shape[dim] // parts).reshape((-1,) + (1,) * (len(shape) - 1 - dim))
    return factor_of


def shared_out(key, own, number, rows, count, top, bound, skew):
    ranking = jax.random.permutation(key, count)
    heavy_load, ordinary = portions_of(count, rows * top, bound, skew, True), portions_of(count, rows * top, bound, skew, False)
    places = jnp.arange(count)

    def named(lengths, turn):
        used = int((lengths > 0).sum())
        fixed = max(1, used // 4)
        shifted = fixed + (places - fixed + turn * (used - fixed)) % max(1, count - fixed)
        return jnp.zeros((count,), jnp.int32).at[ranking[jnp.where(places < fixed, places, shifted)]].set(jnp.asarray(lengths, jnp.int32))

    lengths = jnp.where(number % 4 == 0, named(heavy_load, number // 4), named(ordinary, number - number // 4 - 1))
    mixed = jax.random.permutation(jax.random.fold_in(own, 3), count)
    source_of, sink = mixed[0:count // 2 * 2:2], mixed[1:count // 2 * 2:2]
    room = jnp.minimum(lengths[source_of] - 1, bound - lengths[sink]) // 2
    room = jnp.where((source_of == ranking[0]) | (sink == ranking[0]) | (lengths[sink] == 0), 0, jnp.maximum(room, 0))
    shifted = jax.random.randint(jax.random.fold_in(own, 4), (count // 2,), 0, 1 << 20) % (room + 1)
    lengths = lengths.at[source_of].add(-shifted).at[sink].add(shifted)
    labels = jnp.searchsorted(jnp.cumsum(lengths), jnp.arange(rows * top), side="right").astype(jnp.int32)
    listing = labels.reshape(top, rows).T
    listing = listing[jax.random.permutation(jax.random.fold_in(own, 1), rows)]
    turn = jax.random.randint(jax.random.fold_in(own, 2), (rows, 1), 0, top)
    return jnp.take_along_axis(listing, (jnp.arange(top)[None, :] + turn) % top, axis=1)


def portions_of(amount, total, limit, slope, full):
    loads = [(1 << 20) // math.isqrt(grade ** slope) + 1 for grade in range(1, amount + 1)]
    largest = limit if full else min(limit, max(-(-total // amount), total * loads[0] // sum(loads)))
    least = 1 if total - largest >= amount - 1 else 0
    holding, spare = [largest] + [least] * (amount - 1), total - largest - least * (amount - 1)
    while spare > 0:
        candidates = [i for i in range(1, amount) if holding[i] < largest] or [i for i in range(1, amount) if holding[i] < limit]
        whole, budget = sum([loads[i] for i in candidates]), spare
        for i in candidates:
            more = min(limit - holding[i], max(1, budget * loads[i] // whole), spare)
            holding[i] = holding[i] + more
            spare = spare - more
    return np.array(holding)


def scatter_about(stream_key, dims, spread, reach, cuts=(), kind=jnp.bfloat16):
    gain = shard_levels(stream_key, dims, cuts, -0.22, 0.18) if cuts else 1.0
    result = jax.random.normal(stream_key, dims, jnp.float32) * spread * gain
    return jnp.minimum(jnp.maximum(result, -reach), reach).astype(kind)


def setup_inputs(seed: int = 0) -> dict:
    seeds = jax.random.split(jax.random.key(seed), 8)
    queries = draw_queries(jax.random.fold_in(seeds[7], 71), 0)
    new_keys = draw_new_keys(jax.random.fold_in(seeds[7], 71), 0)
    fresh_values = scatter_about(seeds[2], (TOTAL_TOKENS, KEY_VALUE_HEADS * HEAD_SIZE), 1.0, 6.0, ((0, 64), (1, 4)))
    lent_page_pool = scatter_about(seeds[3], (POOL_SLOTS, 2, PAGE_TOKENS, KEY_VALUE_HEADS * HEAD_SIZE), 1.0, 6.0, ((0, 64), (3, 4)))
    page_lender_keys = jax.random.split(jax.random.fold_in(seeds[4], 1), PAGES // CTX_PAGES)
    page_lender_turns = jax.random.permutation(jax.random.fold_in(seeds[4], 3), PAGES // CTX_PAGES)
    page_lender = jax.vmap(lambda own, number: shared_out(jax.random.fold_in(seeds[4], 2), own, number, CTX_PAGES, N_INST, 1, CAP, 2))(page_lender_keys, page_lender_turns).reshape((PAGES, 1))
    page_slot = set_ends(jax.random.randint(seeds[5], (PAGES,), 0, SLOTS), jax.random.fold_in(seeds[5], 1), 0, SLOTS - 1).astype(jnp.int32)
    starts = draw_starts(jax.random.fold_in(seeds[7], 71), 0)
    return dict(queries=queries, new_keys=new_keys, fresh_values=fresh_values, lent_page_pool=lent_page_pool, page_lender=page_lender, page_slot=page_slot, starts=starts)


def reference(queries, new_keys, fresh_values, lent_page_pool, page_lender, page_slot, starts):
    inst_count = TOTAL_TOKENS // REQUEST_TOKENS
    query_group_width = QUERY_HEADS // KEY_VALUE_HEADS
    page_token_rows = CTX_PAGES * PAGE_TOKENS
    score_scale = 1.0 / math.sqrt(HEAD_SIZE)
    lenders_all = page_lender[:, 0].reshape(inst_count, CTX_PAGES)
    slots_all = page_slot.reshape(inst_count, CTX_PAGES)

    def one_instance(instance):
        local_queries = lax.dynamic_slice_in_dim(queries, instance * REQUEST_TOKENS, REQUEST_TOKENS, 0)
        local_keys = lax.dynamic_slice_in_dim(new_keys, instance * REQUEST_TOKENS, REQUEST_TOKENS, 0)
        local_values = lax.dynamic_slice_in_dim(fresh_values, instance * REQUEST_TOKENS, REQUEST_TOKENS, 0)
        rows_wanted = (lenders_all[instance] * SLOTS + slots_all[instance]).astype(jnp.int32)
        prior_pages = jnp.take(lent_page_pool, rows_wanted, axis=0)
        joined_keys = jnp.concatenate([prior_pages[:, 0].reshape(page_token_rows, KEY_VALUE_HEADS * HEAD_SIZE), local_keys], axis=0)
        joined_values = jnp.concatenate([prior_pages[:, 1].reshape(page_token_rows, KEY_VALUE_HEADS * HEAD_SIZE), local_values], axis=0)
        joined_keys = joined_keys.astype(jnp.float32).reshape(-1, KEY_VALUE_HEADS, HEAD_SIZE)
        joined_values = joined_values.astype(jnp.float32).reshape(-1, KEY_VALUE_HEADS, HEAD_SIZE)
        start_pos = starts[instance]
        context_ok = jnp.broadcast_to((jnp.arange(page_token_rows) < start_pos)[None, :], (REQUEST_TOKENS, page_token_rows))
        causal_ok = jnp.arange(REQUEST_TOKENS)[None, :] <= jnp.arange(REQUEST_TOKENS)[:, None]
        allowed = jnp.concatenate([context_ok, causal_ok], axis=1)
        query_groups = local_queries.astype(jnp.float32).reshape(REQUEST_TOKENS, KEY_VALUE_HEADS, query_group_width, HEAD_SIZE)

        def single_key_head(head_index):
            block_queries = query_groups[:, head_index]
            block_keys = joined_keys[:, head_index]
            block_values = joined_values[:, head_index]
            scores = jnp.einsum('cgd,kd->gck', block_queries, block_keys) * score_scale
            scores = jnp.where(allowed[None], scores, -jnp.inf)
            row_peak = lax.optimization_barrier(jnp.max(scores, axis=2, keepdims=True))
            exponent = jnp.exp(scores - row_peak)
            row_total = lax.optimization_barrier(jnp.sum(exponent, axis=2, keepdims=True))
            weights = lax.optimization_barrier(exponent.astype(jnp.bfloat16)).astype(jnp.float32)
            combined = jnp.einsum('gck,kd->gcd', weights, block_values)
            return combined / row_total
        attention_output = lax.map(single_key_head, jnp.arange(KEY_VALUE_HEADS))
        return attention_output.transpose(2, 0, 1, 3).reshape(REQUEST_TOKENS, QUERY_HEADS * HEAD_SIZE).astype(jnp.bfloat16)
    attention_output = lax.map(one_instance, jnp.arange(inst_count))
    return attention_output.reshape(TOTAL_TOKENS, QUERY_HEADS * HEAD_SIZE)
```

```python
import functools
import math

import jax
import jax.numpy as jnp
from jax import lax
from jax.experimental import pallas as pl
from jax.experimental.pallas import tpu as pltpu
from jax.sharding import PartitionSpec as P

MESH = pl.DeviceIdType.MESH
HEAD = 128
PAGE = 128
NY, NZ, NX = 4, 8, 4
CHIPS = NY * NZ
SLOTS = 16
CTX_PAGES = 32
ROWS = PAGE // NZ
GROUP = 8
KV_HEADS = 2
SCALE = math.log2(math.e) / math.sqrt(HEAD)


def dz_of(i):
    return (i % 2) * ((i + 1) // 2) + (1 - i % 2) * ((NZ - i // 2) % NZ)


def scores(q, k):
    return lax.dot_general(q, k, (((1,), (1,)), ((), ())), preferred_element_type=jnp.float32) * SCALE


def kernel(
    start_ref, q_ref, nk_ref, nv_ref, pool_ref, tab_ref, out_ref,
    stage1, frag, stage2, recv2, tabx, tabj, tabsum, tabs, m_ref, l_ref, acc_ref,
    load_sem, own_sem, smem_sem, xs, xr, ts, tr, s1, r1, fs, fr, s2, r2,
):
    inst, x = lax.axis_index("inst"), lax.axis_index("tp")
    core, chip = inst % 2, inst // 2
    z, y = chip % NZ, chip // NZ
    sibling = (chip * 2 + 1 - core, x)

    def chip_at(i, dy, sign):
        dz = dz_of(i)
        return ((y + sign * dy + NY) % NY) * NZ + (z + sign * dz + NZ) % NZ

    def remote(src, dst, ss, rs, device):
        return pltpu.make_async_remote_copy(
            src_ref=src, dst_ref=dst, send_sem=ss, recv_sem=rs, device_id=device, device_id_type=MESH
        )

    def each(first, body):
        for dy in range(0 if first else 1, NY):
            body(0, dy)

        @pl.loop(1, NZ)
        def _(i):
            for dy in range(NY):
                body(i, dy)

    def load(t):
        yy, zz = t // NZ, t % NZ
        return pltpu.make_async_copy(
            pool_ref.at[:, yy % 2, pl.ds(zz * ROWS, ROWS), pl.ds((yy // 2) * HEAD, HEAD)], stage1.at[t], load_sem
        )

    for t in range(CHIPS):
        load(t).start()

    barrier = pltpu.get_barrier_semaphore()

    def greet(i, dy):
        pl.semaphore_signal(barrier, inc=1, device_id=(chip_at(i, dy, 1) * 2 + core, x), device_id_type=MESH)

    each(False, greet)
    pl.semaphore_signal(barrier, inc=1, device_id=sibling, device_id_type=MESH)
    for d in range(1, NX):
        pl.semaphore_signal(barrier, inc=1, device_id=(inst, (x + d) % NX), device_id_type=MESH)
    pl.semaphore_wait(barrier, CHIPS - 1 + 1 + NX - 1)

    lane = lax.broadcasted_iota(jnp.int32, (8, 128), 1)
    tabx[0] = jnp.where(lane == chip * NX + x, tab_ref[...], 0)

    def table_x(d):
        return remote(tabx.at[0], tabx.at[d], xs.at[d], xr.at[d], (inst, (x + d) % NX))

    for d in range(1, NX):
        table_x(d).start()

    pltpu.make_async_copy(stage1, stage1, load_sem).wait()

    def spread(i, dy):
        t = chip_at(i, dy, 1)
        return remote(
            stage1.at[t], frag.at[pl.ds(inst * SLOTS, SLOTS)], s1.at[i * NY + dy], r1.at[i * NY + dy], (t * 2 + core, x)
        )

    each(False, lambda i, dy: spread(i, dy).start())
    own = pltpu.make_async_copy(stage1.at[chip], frag.at[pl.ds(inst * SLOTS, SLOTS)], own_sem)
    own.start()

    for d in range(1, NX):
        table_x(d).wait()
    tabj[0] = tabx[0] + tabx[1] + tabx[2] + tabx[3]

    def table_j(i, dy):
        s = i * NY + dy
        return remote(tabj.at[0], tabj.at[s], ts.at[s], tr.at[s], (chip_at(i, dy, 1) * 2 + core, x))

    each(False, lambda i, dy: table_j(i, dy).start())

    row = lax.broadcasted_iota(jnp.int32, (PAGE, PAGE), 0)
    col = lax.broadcasted_iota(jnp.int32, (PAGE, PAGE), 1)
    for h in range(KV_HEADS):
        heads = pl.ds(h * HEAD, HEAD)

        @pl.loop(0, GROUP)
        def _(g):
            n = h * GROUP + g
            q = q_ref[:, pl.ds(pl.multiple_of(n * HEAD, HEAD), HEAD)]
            s = jnp.where(col <= row, scores(q, nk_ref[:, heads]), -jnp.inf)
            m = jnp.broadcast_to(jnp.max(s, axis=1, keepdims=True), s.shape)
            p = jnp.exp2(s - m)
            m_ref[n] = m
            l_ref[n] = p
            acc_ref[n] = jnp.dot(p.astype(jnp.bfloat16), nv_ref[:, heads], preferred_element_type=jnp.float32)

    own.wait()

    def forward(i, dy):
        lender = chip_at(i, dy, -1) * 2 + core
        part = frag.at[pl.ds(lender * SLOTS, SLOTS)]
        return remote(part, part, fs.at[i * NY + dy], fr.at[i * NY + dy], sibling)

    def pass_on(i, dy):
        if not (isinstance(i, int) and i == 0 and dy == 0):
            spread(i, dy).wait_recv()
        forward(i, dy).start()

    each(True, pass_on)

    each(False, lambda i, dy: table_j(i, dy).wait())
    total = tabj[0]
    for s in range(1, CHIPS):
        total = total + tabj[s]
    tabsum[...] = total
    to_smem = pltpu.make_async_copy(tabsum, tabs, smem_sem)
    to_smem.start()
    to_smem.wait()

    each(True, lambda i, dy: forward(i, dy).wait())

    def deliver(i, dy):
        s = i * NY + dy
        return remote(stage2.at[s], recv2.at[s], s2.at[s], r2.at[s], (chip_at(i, dy, 1) * 2 + core, x))

    def pick(i, dy):
        s = i * NY + dy
        there = chip_at(i, dy, 1)
        mine = isinstance(i, int) and i == 0 and dy == 0
        for p in range(CTX_PAGES):
            tile = frag[tabs[p % 8, there * NX + p // 8]]
            if mine:
                recv2[0, p] = tile
            else:
                stage2[s, p] = tile
        if not mine:
            deliver(i, dy).start()

    each(False, pick)
    pick(0, 0)

    start = start_ref[0]
    keys = CTX_PAGES * ROWS
    at = lax.broadcasted_iota(jnp.int32, (1, keys), 1)

    def attend(i):
        base = ((z - dz_of(i) + NZ) % NZ) * ROWS
        allowed = at // ROWS * PAGE + at % ROWS + base < start
        for h in range(KV_HEADS):
            k_slot = i * NY + (y - 2 * h + NY) % NY
            v_slot = i * NY + (y - 2 * h - 1 + NY) % NY
            k = recv2[k_slot].reshape(keys, HEAD)
            v = recv2[v_slot].reshape(keys, HEAD)

            @pl.loop(0, GROUP)
            def _(g):
                n = h * GROUP + g
                q = q_ref[:, pl.ds(pl.multiple_of(n * HEAD, HEAD), HEAD)]
                s = jnp.where(allowed, scores(q, k), -jnp.inf)
                parts = [s[:, j * HEAD:(j + 1) * HEAD] for j in range(keys // HEAD)]
                m_old = m_ref[n]
                m = jnp.maximum(m_old, jnp.max(functools.reduce(jnp.maximum, parts), axis=1, keepdims=True))
                alpha = jnp.exp2(m_old - m)
                ps = [jnp.exp2(part - m) for part in parts]
                m_ref[n] = m
                l_ref[n] = l_ref[n] * alpha + functools.reduce(jnp.add, ps)
                p = jnp.concatenate([part.astype(jnp.bfloat16) for part in ps], axis=1)
                acc_ref[n] = acc_ref[n] * alpha + jnp.dot(p, v, preferred_element_type=jnp.float32)

    for dy in range(1, NY):
        deliver(0, dy).wait_recv()
    attend(0)

    @pl.loop(1, NZ)
    def _(i):
        for dy in range(NY):
            deliver(i, dy).wait_recv()
        attend(i)

    for n in range(KV_HEADS * GROUP):
        total = jnp.sum(l_ref[n], axis=1, keepdims=True)
        out_ref[:, n * HEAD:(n + 1) * HEAD] = (acc_ref[n] / total).astype(jnp.bfloat16)

    each(False, lambda i, dy: spread(i, dy).wait_send())
    each(False, lambda i, dy: deliver(i, dy).wait_send())


def local(queries, new_keys, fresh_values, lent_page_pool, page_lender, page_slot, starts):
    pages = page_lender * SLOTS + page_slot[:, None]
    table = jnp.broadcast_to(pages, (8, 128))
    vmem = pl.BlockSpec(memory_space=pltpu.VMEM)
    dma = pltpu.SemaphoreType.DMA
    heads = KV_HEADS * GROUP
    bf16, f32, i32 = jnp.bfloat16, jnp.float32, jnp.int32
    return pl.pallas_call(
        kernel,
        out_shape=jax.ShapeDtypeStruct(queries.shape, bf16),
        in_specs=[
            pl.BlockSpec(memory_space=pltpu.SMEM), vmem, vmem, vmem, pl.BlockSpec(memory_space=pl.ANY), vmem,
        ],
        out_specs=vmem,
        scratch_shapes=[
            pltpu.VMEM((CHIPS, SLOTS, ROWS, HEAD), bf16),
            pltpu.VMEM((CHIPS * 2 * SLOTS, ROWS, HEAD), bf16),
            pltpu.VMEM((CHIPS, CTX_PAGES, ROWS, HEAD), bf16),
            pltpu.VMEM((CHIPS, CTX_PAGES, ROWS, HEAD), bf16),
            pltpu.VMEM((NX, 8, 128), i32),
            pltpu.VMEM((CHIPS, 8, 128), i32),
            pltpu.VMEM((8, 128), i32),
            pltpu.SMEM((8, 128), i32),
            pltpu.VMEM((heads, PAGE, HEAD), f32),
            pltpu.VMEM((heads, PAGE, HEAD), f32),
            pltpu.VMEM((heads, PAGE, HEAD), f32),
            dma, dma, dma,
            dma((NX,)), dma((NX,)),
            dma((CHIPS,)), dma((CHIPS,)),
            dma((CHIPS,)), dma((CHIPS,)),
            dma((CHIPS,)), dma((CHIPS,)),
            dma((CHIPS,)), dma((CHIPS,)),
        ],
        compiler_params=pltpu.CompilerParams(
            collective_id=0, has_side_effects=True, vmem_limit_bytes=48 * 1024 * 1024
        ),
        cost_estimate=pl.CostEstimate(
            flops=4 * heads * PAGE * HEAD * (CTX_PAGES + 1) * PAGE,
            bytes_accessed=4 << 20,
            transcendentals=heads * PAGE * (CTX_PAGES + 1) * PAGE,
        ),
    )(starts, queries, new_keys, fresh_values, lent_page_pool, table)


def solution(mesh):
    in_specs = (
        P("inst", "tp"),
        P("inst", "tp"),
        P("inst", "tp"),
        P("inst", None, None, "tp"),
        P(("inst", "tp"), None),
        P(("inst", "tp")),
        P("inst"),
    )
    return jax.shard_map(local, mesh=mesh, in_specs=in_specs, out_specs=P("inst", "tp"), check_vma=False)
```

```python
import functools
import math

import jax
import jax.numpy as jnp
from jax import lax
from jax.experimental import pallas as pl
from jax.experimental.pallas import tpu as pltpu
from jax.sharding import PartitionSpec as P

MESH = pl.DeviceIdType.MESH
HEAD = 128
PAGE = 128
NY, NZ, NX = 4, 8, 4
CHIPS = NY * NZ
SLOTS = 16
CTX_PAGES = 32
ROWS = PAGE // NZ
GROUP = 8
KV_HEADS = 2
UNROLL = 1
PAIR = 8
SCALE = math.log2(math.e) / math.sqrt(HEAD)


def dz_of(i):
    return (i % 2) * ((i + 1) // 2) + (1 - i % 2) * ((NZ - i // 2) % NZ)


def scores(q, k):
    return lax.dot_general(q, k, (((1,), (1,)), ((), ())), preferred_element_type=jnp.float32) * SCALE


def wide_kernel(
    start_ref, q_ref, nk_ref, nv_ref, pool_ref, tab_ref, out_ref,
    stage1, frag, stage2, recv2, tabx, tabj, tabsum, tabs, m_ref, l_ref, acc_ref,
    load_sem, own_sem, smem_sem, xs, xr, ts, tr, s1, r1, fs, fr, s2, r2,
):
    inst, x = lax.axis_index("inst"), lax.axis_index("tp")
    core, chip = inst % 2, inst // 2
    z, y = chip % NZ, chip // NZ
    sibling = (chip * 2 + 1 - core, x)

    def chip_at(i, dy, sign):
        dz = dz_of(i)
        return ((y + sign * dy + NY) % NY) * NZ + (z + sign * dz + NZ) % NZ

    def remote(src, dst, ss, rs, device):
        return pltpu.make_async_remote_copy(
            src_ref=src, dst_ref=dst, send_sem=ss, recv_sem=rs, device_id=device, device_id_type=MESH
        )

    def each(first, body):
        for dy in range(0 if first else 1, NY):
            body(0, dy)

        @pl.loop(1, NZ)
        def _(i):
            for dy in range(NY):
                body(i, dy)

    def load(t):
        yy, zz = t // NZ, t % NZ
        return pltpu.make_async_copy(
            pool_ref.at[:, yy % 2, pl.ds(zz * ROWS, ROWS), pl.ds((yy // 2) * HEAD, HEAD)], stage1.at[t], load_sem
        )

    for t in range(CHIPS):
        load(t).start()

    barrier = pltpu.get_barrier_semaphore()

    def greet(i, dy):
        pl.semaphore_signal(barrier, inc=1, device_id=(chip_at(i, dy, 1) * 2 + core, x), device_id_type=MESH)

    each(False, greet)
    pl.semaphore_signal(barrier, inc=1, device_id=sibling, device_id_type=MESH)
    for d in range(1, NX):
        pl.semaphore_signal(barrier, inc=1, device_id=(inst, (x + d) % NX), device_id_type=MESH)
    pl.semaphore_wait(barrier, CHIPS - 1 + 1 + NX - 1)

    lane = lax.broadcasted_iota(jnp.int32, (8, 128), 1)
    tabx[0] = jnp.where(lane == chip * NX + x, tab_ref[...], 0)

    def table_x(d):
        return remote(tabx.at[0], tabx.at[d], xs.at[d], xr.at[d], (inst, (x + d) % NX))

    for d in range(1, NX):
        table_x(d).start()

    pltpu.make_async_copy(stage1, stage1, load_sem).wait()

    def spread(i, dy):
        t = chip_at(i, dy, 1)
        return remote(
            stage1.at[t], frag.at[pl.ds(inst * SLOTS, SLOTS)], s1.at[i * NY + dy], r1.at[i * NY + dy], (t * 2 + core, x)
        )

    each(False, lambda i, dy: spread(i, dy).start())
    own = pltpu.make_async_copy(stage1.at[chip], frag.at[pl.ds(inst * SLOTS, SLOTS)], own_sem)
    own.start()

    for d in range(1, NX):
        table_x(d).wait()
    tabj[0] = tabx[0] + tabx[1] + tabx[2] + tabx[3]

    def table_j(i, dy):
        s = i * NY + dy
        return remote(tabj.at[0], tabj.at[s], ts.at[s], tr.at[s], (chip_at(i, dy, 1) * 2 + core, x))

    each(False, lambda i, dy: table_j(i, dy).start())

    row = lax.broadcasted_iota(jnp.int32, (PAGE, PAGE), 0)
    col = lax.broadcasted_iota(jnp.int32, (PAGE, PAGE), 1)
    for h in range(KV_HEADS):
        heads = pl.ds(h * HEAD, HEAD)

        @pl.loop(0, GROUP)
        def _(g):
            n = h * GROUP + g
            q = q_ref[:, pl.ds(pl.multiple_of(n * HEAD, HEAD), HEAD)]
            s = jnp.where(col <= row, scores(q, nk_ref[:, heads]), -jnp.inf)
            m = jnp.broadcast_to(jnp.max(s, axis=1, keepdims=True), s.shape)
            p = jnp.exp2(s - m)
            m_ref[n] = m
            l_ref[n] = p
            acc_ref[n] = jnp.dot(p.astype(jnp.bfloat16), nv_ref[:, heads], preferred_element_type=jnp.float32)

    own.wait()

    def forward(i, dy):
        lender = chip_at(i, dy, -1) * 2 + core
        part = frag.at[pl.ds(lender * SLOTS, SLOTS)]
        return remote(part, part, fs.at[i * NY + dy], fr.at[i * NY + dy], sibling)

    def pass_on(i, dy):
        if not (isinstance(i, int) and i == 0 and dy == 0):
            spread(i, dy).wait_recv()
        forward(i, dy).start()

    each(True, pass_on)

    each(False, lambda i, dy: table_j(i, dy).wait())
    total = tabj[0]
    for s in range(1, CHIPS):
        total = total + tabj[s]
    tabsum[...] = total
    to_smem = pltpu.make_async_copy(tabsum, tabs, smem_sem)
    to_smem.start()
    to_smem.wait()

    each(True, lambda i, dy: forward(i, dy).wait())

    def deliver(i, dy):
        s = i * NY + dy
        return remote(stage2.at[s], recv2.at[s], s2.at[s], r2.at[s], (chip_at(i, dy, 1) * 2 + core, x))

    def pick(i, dy):
        s = i * NY + dy
        there = chip_at(i, dy, 1)
        mine = isinstance(i, int) and i == 0 and dy == 0
        for p in range(CTX_PAGES):
            tile = frag[tabs[p % 8, there * NX + p // 8]]
            if mine:
                recv2[0, p] = tile
            else:
                stage2[s, p] = tile
        if not mine:
            deliver(i, dy).start()

    each(False, pick)
    pick(0, 0)

    start = start_ref[0]
    keys = CTX_PAGES * ROWS
    at = lax.broadcasted_iota(jnp.int32, (1, keys), 1)

    def attend(i):
        base = ((z - dz_of(i) + NZ) % NZ) * ROWS
        allowed = at // ROWS * PAGE + at % ROWS + base < start
        for h in range(KV_HEADS):
            k_slot = i * NY + (y - 2 * h + NY) % NY
            v_slot = i * NY + (y - 2 * h - 1 + NY) % NY
            k = recv2[k_slot].reshape(keys, HEAD)
            v = recv2[v_slot].reshape(keys, HEAD)

            @pl.loop(0, GROUP)
            def _(g):
                n = h * GROUP + g
                q = q_ref[:, pl.ds(pl.multiple_of(n * HEAD, HEAD), HEAD)]
                s = jnp.where(allowed, scores(q, k), -jnp.inf)
                parts = [s[:, j * HEAD:(j + 1) * HEAD] for j in range(keys // HEAD)]
                m_old = m_ref[n]
                m = jnp.maximum(m_old, jnp.max(functools.reduce(jnp.maximum, parts), axis=1, keepdims=True))
                alpha = jnp.exp2(m_old - m)
                ps = [jnp.exp2(part - m) for part in parts]
                m_ref[n] = m
                l_ref[n] = l_ref[n] * alpha + functools.reduce(jnp.add, ps)
                p = jnp.concatenate([part.astype(jnp.bfloat16) for part in ps], axis=1)
                acc_ref[n] = acc_ref[n] * alpha + jnp.dot(p, v, preferred_element_type=jnp.float32)

    for dy in range(1, NY):
        deliver(0, dy).wait_recv()
    attend(0)

    @pl.loop(1, NZ)
    def _(i):
        for dy in range(NY):
            deliver(i, dy).wait_recv()
        attend(i)

    for n in range(KV_HEADS * GROUP):
        total = jnp.sum(l_ref[n], axis=1, keepdims=True)
        out_ref[:, n * HEAD:(n + 1) * HEAD] = (acc_ref[n] / total).astype(jnp.bfloat16)

    each(False, lambda i, dy: spread(i, dy).wait_send())
    each(False, lambda i, dy: deliver(i, dy).wait_send())


ROUNDS = 4
OPEN = 2
PLANE = 2 * NY * SLOTS
WIDTH = (84, 72, 56, 24)
OFF = (0, 128, 200, 256)
TOTAL = OFF[-1] + WIDTH[-1]
JOINED = PLANE + 2 * TOTAL
HOPS = len(WIDTH)
STEP = (1, -1)


def width(r, t):
    return PLANE if t == 1 and r < OPEN else WIDTH[t - 1]


def base_of(s, t):
    return PLANE + s * TOTAL + OFF[t - 1]


def narrow_kernel(
    start_ref, tab_ref, q_any, nk_any, nv_any, pool_ref, out_ref, over_ref,
    q_ref, nk_ref, nv_ref, stage, home, arrive, sbuf, join, ybuf, recv,
    tabx, tabz, tabp, tabv, tabs, need, member, before, place, mat, metav, meta, plist, m_ref, l_ref, acc_ref,
    in_sem, load_sem, own_sem, smem_sem, xs, xr, zs, zr, ps, pr, hs, hr, rs, rr, ys, yr,
):
    inst, x = lax.axis_index("inst"), lax.axis_index("tp")
    core, chip = inst % 2, inst // 2
    z, y = chip % NZ, chip // NZ
    i32 = jnp.int32

    def device(dy, dz, dc):
        return ((((y + dy) % NY) * NZ + (z + dz + NZ) % NZ) * 2 + (core + dc) % 2, x)

    def remote(src, dst, ss, rs_, dev):
        return pltpu.make_async_remote_copy(
            src_ref=src, dst_ref=dst, send_sem=ss, recv_sem=rs_, device_id=dev, device_id_type=MESH
        )

    inputs = [
        pltpu.make_async_copy(src, dst, in_sem.at[n])
        for n, (src, dst) in enumerate(((q_any, q_ref), (nk_any, nk_ref), (nv_any, nv_ref)))
    ]
    for yy in range(NY):
        for tb in range(NZ):
            pltpu.make_async_copy(
                pool_ref.at[:, yy % 2, pl.ds(tb * ROWS, ROWS), pl.ds((yy // 2) * HEAD, HEAD)],
                stage.at[yy, tb % 2, tb // 2], load_sem,
            ).start()
    for copy in inputs:
        copy.start()

    barrier = pltpu.get_barrier_semaphore()

    def greet(dev):
        pl.semaphore_signal(barrier, inc=1, device_id=dev, device_id_type=MESH)

    for d in range(1, NX):
        greet((inst, (x + d) % NX))

    @pl.loop(1, NZ)
    def _(d):
        greet(device(0, d, 0))

    @pl.loop(1, 2 * NY)
    def _(k):
        greet(device(k // 2, 0, k % 2))

    pl.semaphore_wait(barrier, NX - 1 + NZ - 1 + 2 * NY - 1)

    row = lax.broadcasted_iota(i32, (8, 128), 0)
    lane = lax.broadcasted_iota(i32, (8, 128), 1)
    wanted = (lane == chip * NX + x) & ((x * 8 + row) * PAGE < start_ref[0])
    tabx[0] = jnp.where(wanted, tab_ref[...], 0)

    def table_x(d):
        return remote(tabx.at[0], tabx.at[d], xs.at[d], xr.at[d], (inst, (x + d) % NX))

    for d in range(1, NX):
        table_x(d).start()

    pltpu.make_async_copy(stage, stage, load_sem).wait()
    here = pl.ds((y * 2 + core) * SLOTS, SLOTS)

    def spread(r, k):
        dy, dc = k // 2, k % 2
        return remote(
            stage.at[(y + dy) % NY, (core + dc) % 2, r], home[r].at[here], hs.at[r, k], hr.at[r, k], device(dy, 0, dc)
        )

    def own(r):
        return pltpu.make_async_copy(stage.at[y, core, r], home[r].at[here], own_sem.at[r])

    def spread_all(r):
        own(r).start()

        @pl.loop(1, 2 * NY)
        def _(k):
            spread(r, k).start()

    def hop(r, s, t):
        src = home[r] if width(r, t) == PLANE else sbuf.at[r, s, pl.ds(OFF[t - 1], WIDTH[t - 1])]
        return remote(src, arrive[r][s][t - 1], rs.at[r, s, t - 1], rr.at[r, s, t - 1], device(0, STEP[s], 0))

    def ring(r, t):
        if t == 1:
            own(r).wait()

            @pl.loop(1, 2 * NY)
            def _(k):
                spread(r, k).wait_recv()

        lists = 3 if r < OPEN else 1
        for s in range(2):
            source = home[r]
            if t > 1:
                hop(r, s, t - 1).wait_recv()
                source = arrive[r][s][t - 2]
            if width(r, t) < PLANE:

                @pl.loop(0, WIDTH[t - 1] // 4)
                def _(kk):
                    for u in range(4):
                        k = kk * 4 + u
                        sbuf[r, s, OFF[t - 1] + k] = source[meta[lists, s * HOPS + t - 1, k]]

            hop(r, s, t).start()

    spread_all(0)

    for d in range(1, NX):
        table_x(d).wait()
    tabz[0] = tabx[0] + tabx[1] + tabx[2] + tabx[3]

    def table_z(d):
        return remote(tabz.at[0], tabz.at[d], zs.at[d], zr.at[d], device(0, d, 0))

    @pl.loop(1, NZ)
    def _(d):
        table_z(d).start()

    @pl.loop(1, NZ)
    def _(d):
        table_z(d).wait()

    tabp[0] = functools.reduce(jnp.add, [tabz[d] for d in range(NZ)])

    def table_p(k):
        return remote(tabp.at[0], tabp.at[k], ps.at[k], pr.at[k], device(k // 2, 0, k % 2))

    @pl.loop(1, 2 * NY)
    def _(k):
        table_p(k).start()

    spread_all(1)
    ring(0, 1)

    @pl.loop(1, 2 * NY)
    def _(k):
        table_p(k).wait()

    for dc in range(2):
        tabv[dc] = functools.reduce(jnp.add, [tabp[2 * dy + dc] for dy in range(NY)])
    to_smem = pltpu.make_async_copy(tabv, tabs, smem_sem.at[0])
    to_smem.start()
    ring(1, 1)
    for r in range(2, ROUNDS):
        spread_all(r)
    to_smem.wait()

    number = row * PLANE + lane + 1

    @pl.loop(0, NZ)
    def _(d):
        hit = jnp.zeros((8, 128), i32)
        for dc in range(2):
            for yy in range(NY):
                for xx in range(NX):
                    for e in range(8):
                        hit = jnp.where(number == tabs[dc, e, (yy * NZ + d) * NX + xx], 1, hit)
        need[d] = hit

    def ahead(k):
        return functools.reduce(jnp.add, [jnp.where(row == (d - k) % NZ, need[d], 0) for d in range(NZ)])

    even = lane % 2 == 0
    far = ahead(NZ // 2)
    over = None
    for s in range(2):
        users = [jnp.where(even if s == 0 else ~even, far, 0)]
        for t in range(HOPS - 1, 0, -1):
            users.insert(0, users[0] | ahead(t if s == 0 else NZ - t))
        for t in range(1, HOPS + 1):
            n = s * HOPS + t - 1
            count = users[t - 1]
            shift = 1
            while shift < 128:
                count = count + jnp.where(lane >= shift, pltpu.roll(count, shift, 1), 0)
                shift *= 2
            excess = count - WIDTH[t - 1]
            over = excess if over is None else jnp.maximum(over, excess)
            count = count - users[t - 1]
            member[n] = users[t - 1]
            before[n] = count
            place[n] = jnp.minimum(count, WIDTH[t - 1] - 1)
    over_ref[0, 0] = jnp.max(over)

    for variant in range(2):
        where_to = jnp.where(row == z, lane, 0)
        for s in range(2):
            for t in range(1, HOPS + 1):
                mine = row == (z - STEP[s] * t + NZ) % NZ
                if t == HOPS:
                    mine = mine & (even if s == 0 else ~even)
                at_hop = lane if variant and t == 1 else place[s * HOPS + t - 1]
                where_to = where_to + jnp.where(mine, base_of(s, t) + at_hop, 0)
        metav[2 * variant] = where_to

    mat[...] = jnp.zeros_like(mat)
    for s in range(2):
        for t in range(1, HOPS + 1):
            n = s * HOPS + t - 1
            o = pl.ds((z - STEP[s] * (t - 1) + NZ) % NZ, 1)
            mat[n:n + 1] = jnp.where(member[n, o] > 0, before[n, o], 999)
            mat[8 + n:9 + n] = lane[0:1] if t == 1 else place[n - 1, o]
    turned = mat[...].T
    lanes = lax.broadcasted_iota(i32, (128, 128), 1)
    pages = lax.broadcasted_iota(i32, (128, 128), 0)
    for n in range(2 * HOPS):
        goes = turned[:, n:n + 1] == lanes
        row_n = jnp.sum(jnp.where(goes, turned[:, 8 + n:9 + n], 0), axis=0, keepdims=True)
        metav[1, n:n + 1] = row_n
        if n % HOPS == 1:
            row_n = jnp.sum(jnp.where(goes, pages, 0), axis=0, keepdims=True)
        metav[3, n:n + 1] = row_n
    to_smem2 = pltpu.make_async_copy(metav, meta, smem_sem.at[1])
    to_smem2.start()
    to_smem2.wait()

    def find():
        @pl.loop(0, 2 * NY)
        def _(k):
            column = (((y + k // 2) % NY) * NZ + z) * NX
            for p in range(CTX_PAGES):
                e = jnp.maximum(tabs[k % 2, p % 8, column + p // 8] - 1, 0)
                for variant in range(2):
                    plist[variant * 2 * NY + k, p] = meta[2 * variant, e // PLANE, e % PLANE]

    def deliver(r, k):
        return remote(ybuf.at[r, k], recv.at[r, k], ys.at[r, k], yr.at[r, k], device(k // 2, 0, k % 2))

    def hand_out(r):
        for s in range(2):
            hop(r, s, HOPS).wait_recv()

        @pl.loop(0, PLANE // 8)
        def _(j):
            join[pl.ds(j * 8, 8)] = home[r][pl.ds(j * 8, 8)]

        for s in range(2):
            for t in range(1, HOPS + 1):

                @pl.loop(0, width(r, t) // 4)
                def _(j):
                    join[pl.ds(base_of(s, t) + j * 4, 4)] = arrive[r][s][t - 1][pl.ds(j * 4, 4)]

        lists = 2 * NY if r < OPEN else 0

        def pick(k):
            for p in range(CTX_PAGES):
                ybuf[r, k, p] = join[plist[lists + k, p]]
            deliver(r, k).start()

        @pl.loop(1, NY)
        def _(dy):
            pick(2 * dy)

        @pl.loop(0, NY)
        def _(dy):
            pick(2 * dy + 1)

        for p in range(CTX_PAGES):
            recv[r, 0, p] = join[plist[lists, p]]

    def new_tokens():
        for copy in inputs:
            copy.wait()
        rows_ = lax.broadcasted_iota(i32, (PAGE, PAGE), 0)
        cols_ = lax.broadcasted_iota(i32, (PAGE, PAGE), 1)
        for h in range(KV_HEADS):
            heads = pl.ds(h * HEAD, HEAD)

            @pl.loop(0, GROUP, unroll=UNROLL)
            def _(g):
                n = h * GROUP + g
                q = q_ref[:, pl.ds(pl.multiple_of(n * HEAD, HEAD), HEAD)]
                s = jnp.where(cols_ <= rows_, scores(q, nk_ref[:, heads]), -jnp.inf)
                m = jnp.broadcast_to(jnp.max(s, axis=1, keepdims=True), s.shape)
                p = jnp.exp2(s - m)
                m_ref[n] = m
                l_ref[n] = p
                acc_ref[n] = jnp.dot(p.astype(jnp.bfloat16), nv_ref[:, heads], preferred_element_type=jnp.float32)

    start = start_ref[0]
    keys = CTX_PAGES * ROWS
    at = lax.broadcasted_iota(i32, (1, keys), 1)

    def attend(r, dc, h):
        tb = 2 * r + (core + dc) % 2
        allowed = at // ROWS * PAGE + at % ROWS + tb * ROWS < start
        k = recv[r, (y - 2 * h + NY) % NY * 2 + dc].reshape(keys, HEAD)
        v = recv[r, (y - 2 * h - 1 + NY) % NY * 2 + dc].reshape(keys, HEAD)

        @pl.loop(0, GROUP // PAIR, unroll=UNROLL)
        def _(g):
            n = h * GROUP + g * PAIR
            wide_row = (PAIR * PAGE, HEAD)
            q = jnp.concatenate(
                [q_ref[:, pl.ds(pl.multiple_of((n + e) * HEAD, HEAD), HEAD)] for e in range(PAIR)], axis=0
            )
            s = jnp.where(allowed, scores(q, k), -jnp.inf)
            parts = [s[:, j * HEAD:(j + 1) * HEAD] for j in range(keys // HEAD)]
            m_old = m_ref[pl.ds(n, PAIR)].reshape(wide_row)
            m = jnp.maximum(m_old, jnp.max(functools.reduce(jnp.maximum, parts), axis=1, keepdims=True))
            alpha = jnp.exp2(m_old - m)
            ps_ = [jnp.exp2(part - m) for part in parts]
            m_ref[pl.ds(n, PAIR)] = m.reshape(PAIR, PAGE, HEAD)
            l = l_ref[pl.ds(n, PAIR)].reshape(wide_row) * alpha + functools.reduce(jnp.add, ps_)
            l_ref[pl.ds(n, PAIR)] = l.reshape(PAIR, PAGE, HEAD)
            p = jnp.concatenate([part.astype(jnp.bfloat16) for part in ps_], axis=1)
            acc = acc_ref[pl.ds(n, PAIR)].reshape(wide_row) * alpha
            acc = acc + jnp.dot(p, v, preferred_element_type=jnp.float32)
            acc_ref[pl.ds(n, PAIR)] = acc.reshape(PAIR, PAGE, HEAD)

    def units(r, first, last):
        for dc in range(2):
            if first <= 2 * dc < last:

                @pl.loop(1 - dc, NY)
                def _(dy):
                    deliver(r, 2 * dy + dc).wait_recv()

            lo, hi = max(first, 2 * dc), min(last, 2 * dc + 2)
            if lo < hi:

                @pl.loop(lo - 2 * dc, hi - 2 * dc)
                def _(h):
                    attend(r, dc, h)

    find()
    new_tokens()
    ring(0, 2)
    ring(2, 1)
    ring(0, 3)
    ring(1, 2)
    ring(3, 1)
    ring(0, 4)
    ring(1, 3)
    ring(2, 2)
    hand_out(0)
    ring(1, 4)
    ring(2, 3)
    units(0, 0, 2)
    hand_out(1)
    ring(3, 2)
    units(0, 2, 4)
    ring(2, 4)
    units(1, 0, 1)
    ring(3, 3)
    units(1, 1, 2)
    hand_out(2)
    ring(3, 4)
    units(1, 2, 4)
    hand_out(3)
    units(2, 0, 4)
    units(3, 0, 4)

    for n in range(KV_HEADS * GROUP):
        total = jnp.sum(l_ref[n], axis=1, keepdims=True)
        out_ref[:, n * HEAD:(n + 1) * HEAD] = (acc_ref[n] / total).astype(jnp.bfloat16)

    for r in range(ROUNDS):

        @pl.loop(1, 2 * NY)
        def _(k):
            spread(r, k).wait_send()
            deliver(r, k).wait_send()

        for s in range(2):
            for t in range(1, HOPS + 1):
                hop(r, s, t).wait_send()


def narrow(queries, new_keys, fresh_values, lent_page_pool, page_lender, page_slot, starts):
    lender = page_lender[:, 0]
    page = (lender // 2 % NZ) * PLANE + (lender // (2 * NZ) * 2 + lender % 2) * SLOTS + page_slot
    table = jnp.broadcast_to(page[:, None] + 1, (8, 128))
    vmem, smem, hbm = (pl.BlockSpec(memory_space=space) for space in (pltpu.VMEM, pltpu.SMEM, pl.ANY))
    dma = pltpu.SemaphoreType.DMA
    heads = KV_HEADS * GROUP
    bf16, f32, i32 = jnp.bfloat16, jnp.float32, jnp.int32
    tiles = lambda *n: pltpu.VMEM((*n, ROWS, HEAD), bf16)
    ints = lambda *n: pltpu.VMEM((*n, 8, 128), i32)
    return pl.pallas_call(
        narrow_kernel,
        out_shape=(jax.ShapeDtypeStruct(queries.shape, bf16), jax.ShapeDtypeStruct((1, 1), i32)),
        in_specs=[smem, vmem, hbm, hbm, hbm, hbm],
        out_specs=(vmem, smem),
        scratch_shapes=[
            pltpu.VMEM(queries.shape, bf16), pltpu.VMEM(new_keys.shape, bf16), pltpu.VMEM(fresh_values.shape, bf16),
            tiles(NY, 2, ROUNDS, SLOTS),
            [tiles(PLANE) for _ in range(ROUNDS)],
            [[[tiles(width(r, t + 1)) for t in range(HOPS)] for _ in range(2)] for r in range(ROUNDS)],
            tiles(ROUNDS, 2, TOTAL), tiles(JOINED),
            tiles(ROUNDS, 2 * NY, CTX_PAGES), tiles(ROUNDS, 2 * NY, CTX_PAGES),
            ints(NX), ints(NZ), ints(2 * NY), ints(2), pltpu.SMEM((2, 8, 128), i32),
            ints(NZ), ints(2 * HOPS), ints(2 * HOPS), ints(2 * HOPS), pltpu.VMEM((128, 128), i32),
            ints(4), pltpu.SMEM((4, 8, 128), i32), pltpu.SMEM((16, 128), i32),
            pltpu.VMEM((heads, PAGE, HEAD), f32), pltpu.VMEM((heads, PAGE, HEAD), f32), pltpu.VMEM((heads, PAGE, HEAD), f32),
            dma((3,)), dma, dma((ROUNDS,)), dma((2,)),
            dma((NX,)), dma((NX,)), dma((NZ,)), dma((NZ,)), dma((2 * NY,)), dma((2 * NY,)),
            dma((ROUNDS, 2 * NY)), dma((ROUNDS, 2 * NY)),
            dma((ROUNDS, 2, HOPS)), dma((ROUNDS, 2, HOPS)),
            dma((ROUNDS, 2 * NY)), dma((ROUNDS, 2 * NY)),
        ],
        compiler_params=pltpu.CompilerParams(
            collective_id=1, has_side_effects=True, vmem_limit_bytes=56 * 1024 * 1024
        ),
        cost_estimate=pl.CostEstimate(
            flops=4 * heads * PAGE * HEAD * (CTX_PAGES + 1) * PAGE,
            bytes_accessed=4 << 20,
            transcendentals=heads * PAGE * (CTX_PAGES + 1) * PAGE,
        ),
    )(starts, table, queries, new_keys, fresh_values, lent_page_pool)


def wide(queries, new_keys, fresh_values, lent_page_pool, page_lender, page_slot, starts):
    pages = page_lender * SLOTS + page_slot[:, None]
    table = jnp.broadcast_to(pages, (8, 128))
    vmem = pl.BlockSpec(memory_space=pltpu.VMEM)
    dma = pltpu.SemaphoreType.DMA
    heads = KV_HEADS * GROUP
    bf16, f32, i32 = jnp.bfloat16, jnp.float32, jnp.int32
    return pl.pallas_call(
        wide_kernel,
        out_shape=jax.ShapeDtypeStruct(queries.shape, bf16),
        in_specs=[
            pl.BlockSpec(memory_space=pltpu.SMEM), vmem, vmem, vmem, pl.BlockSpec(memory_space=pl.ANY), vmem,
        ],
        out_specs=vmem,
        scratch_shapes=[
            pltpu.VMEM((CHIPS, SLOTS, ROWS, HEAD), bf16),
            pltpu.VMEM((CHIPS * 2 * SLOTS, ROWS, HEAD), bf16),
            pltpu.VMEM((CHIPS, CTX_PAGES, ROWS, HEAD), bf16),
            pltpu.VMEM((CHIPS, CTX_PAGES, ROWS, HEAD), bf16),
            pltpu.VMEM((NX, 8, 128), i32),
            pltpu.VMEM((CHIPS, 8, 128), i32),
            pltpu.VMEM((8, 128), i32),
            pltpu.SMEM((8, 128), i32),
            pltpu.VMEM((heads, PAGE, HEAD), f32),
            pltpu.VMEM((heads, PAGE, HEAD), f32),
            pltpu.VMEM((heads, PAGE, HEAD), f32),
            dma, dma, dma,
            dma((NX,)), dma((NX,)),
            dma((CHIPS,)), dma((CHIPS,)),
            dma((CHIPS,)), dma((CHIPS,)),
            dma((CHIPS,)), dma((CHIPS,)),
            dma((CHIPS,)), dma((CHIPS,)),
        ],
        compiler_params=pltpu.CompilerParams(
            collective_id=0, has_side_effects=True, vmem_limit_bytes=48 * 1024 * 1024
        ),
        cost_estimate=pl.CostEstimate(
            flops=4 * heads * PAGE * HEAD * (CTX_PAGES + 1) * PAGE,
            bytes_accessed=4 << 20,
            transcendentals=heads * PAGE * (CTX_PAGES + 1) * PAGE,
        ),
    )(starts, queries, new_keys, fresh_values, lent_page_pool, table)


def local(*args):
    out, over = narrow(*args)
    return lax.cond(over[0, 0] > 0, lambda: wide(*args), lambda: out)


def solution(mesh):
    in_specs = (
        P("inst", "tp"),
        P("inst", "tp"),
        P("inst", "tp"),
        P("inst", None, None, "tp"),
        P(("inst", "tp"), None),
        P(("inst", "tp")),
        P("inst"),
    )
    return jax.shard_map(local, mesh=mesh, in_specs=in_specs, out_specs=P("inst", "tp"), check_vma=False)
```

```python
import functools
import math

import jax
import jax.numpy as jnp
from jax import lax
from jax.experimental import pallas as pl
from jax.experimental.pallas import tpu as pltpu
from jax.sharding import PartitionSpec as P

MESH = pl.DeviceIdType.MESH
HEAD = 128
PAGE = 128
NY, NZ, NX = 4, 8, 4
CHIPS = NY * NZ
SLOTS = 16
CTX_PAGES = 32
ROWS = PAGE // NZ
GROUP = 8
KV_HEADS = 2
UNROLL = 1
PAIR = 8
SCALE = math.log2(math.e) / math.sqrt(HEAD)


def dz_of(i):
    return (i % 2) * ((i + 1) // 2) + (1 - i % 2) * ((NZ - i // 2) % NZ)


def scores(q, k):
    return lax.dot_general(q, k, (((1,), (1,)), ((), ())), preferred_element_type=jnp.float32) * SCALE


def wide_kernel(
    start_ref, q_ref, nk_ref, nv_ref, pool_ref, tab_ref, out_ref,
    stage1, frag, stage2, recv2, tabx, tabj, tabsum, tabs, m_ref, l_ref, acc_ref,
    load_sem, own_sem, smem_sem, xs, xr, ts, tr, s1, r1, fs, fr, s2, r2,
):
    inst, x = lax.axis_index("inst"), lax.axis_index("tp")
    core, chip = inst % 2, inst // 2
    z, y = chip % NZ, chip // NZ
    sibling = (chip * 2 + 1 - core, x)

    def chip_at(i, dy, sign):
        dz = dz_of(i)
        return ((y + sign * dy + NY) % NY) * NZ + (z + sign * dz + NZ) % NZ

    def remote(src, dst, ss, rs, device):
        return pltpu.make_async_remote_copy(
            src_ref=src, dst_ref=dst, send_sem=ss, recv_sem=rs, device_id=device, device_id_type=MESH
        )

    def each(first, body):
        for dy in range(0 if first else 1, NY):
            body(0, dy)

        @pl.loop(1, NZ)
        def _(i):
            for dy in range(NY):
                body(i, dy)

    def load(t):
        yy, zz = t // NZ, t % NZ
        return pltpu.make_async_copy(
            pool_ref.at[:, yy % 2, pl.ds(zz * ROWS, ROWS), pl.ds((yy // 2) * HEAD, HEAD)], stage1.at[t], load_sem
        )

    for t in range(CHIPS):
        load(t).start()

    barrier = pltpu.get_barrier_semaphore()

    def greet(i, dy):
        pl.semaphore_signal(barrier, inc=1, device_id=(chip_at(i, dy, 1) * 2 + core, x), device_id_type=MESH)

    each(False, greet)
    pl.semaphore_signal(barrier, inc=1, device_id=sibling, device_id_type=MESH)
    for d in range(1, NX):
        pl.semaphore_signal(barrier, inc=1, device_id=(inst, (x + d) % NX), device_id_type=MESH)
    pl.semaphore_wait(barrier, CHIPS - 1 + 1 + NX - 1)

    lane = lax.broadcasted_iota(jnp.int32, (8, 128), 1)
    tabx[0] = jnp.where(lane == chip * NX + x, tab_ref[...], 0)

    def table_x(d):
        return remote(tabx.at[0], tabx.at[d], xs.at[d], xr.at[d], (inst, (x + d) % NX))

    for d in range(1, NX):
        table_x(d).start()

    pltpu.make_async_copy(stage1, stage1, load_sem).wait()

    def spread(i, dy):
        t = chip_at(i, dy, 1)
        return remote(
            stage1.at[t], frag.at[pl.ds(inst * SLOTS, SLOTS)], s1.at[i * NY + dy], r1.at[i * NY + dy], (t * 2 + core, x)
        )

    each(False, lambda i, dy: spread(i, dy).start())
    own = pltpu.make_async_copy(stage1.at[chip], frag.at[pl.ds(inst * SLOTS, SLOTS)], own_sem)
    own.start()

    for d in range(1, NX):
        table_x(d).wait()
    tabj[0] = tabx[0] + tabx[1] + tabx[2] + tabx[3]

    def table_j(i, dy):
        s = i * NY + dy
        return remote(tabj.at[0], tabj.at[s], ts.at[s], tr.at[s], (chip_at(i, dy, 1) * 2 + core, x))

    each(False, lambda i, dy: table_j(i, dy).start())

    row = lax.broadcasted_iota(jnp.int32, (PAGE, PAGE), 0)
    col = lax.broadcasted_iota(jnp.int32, (PAGE, PAGE), 1)
    for h in range(KV_HEADS):
        heads = pl.ds(h * HEAD, HEAD)

        @pl.loop(0, GROUP)
        def _(g):
            n = h * GROUP + g
            q = q_ref[:, pl.ds(pl.multiple_of(n * HEAD, HEAD), HEAD)]
            s = jnp.where(col <= row, scores(q, nk_ref[:, heads]), -jnp.inf)
            m = jnp.broadcast_to(jnp.max(s, axis=1, keepdims=True), s.shape)
            p = jnp.exp2(s - m)
            m_ref[n] = m
            l_ref[n] = p
            acc_ref[n] = jnp.dot(p.astype(jnp.bfloat16), nv_ref[:, heads], preferred_element_type=jnp.float32)

    own.wait()

    def forward(i, dy):
        lender = chip_at(i, dy, -1) * 2 + core
        part = frag.at[pl.ds(lender * SLOTS, SLOTS)]
        return remote(part, part, fs.at[i * NY + dy], fr.at[i * NY + dy], sibling)

    def pass_on(i, dy):
        if not (isinstance(i, int) and i == 0 and dy == 0):
            spread(i, dy).wait_recv()
        forward(i, dy).start()

    each(True, pass_on)

    each(False, lambda i, dy: table_j(i, dy).wait())
    total = tabj[0]
    for s in range(1, CHIPS):
        total = total + tabj[s]
    tabsum[...] = total
    to_smem = pltpu.make_async_copy(tabsum, tabs, smem_sem)
    to_smem.start()
    to_smem.wait()

    each(True, lambda i, dy: forward(i, dy).wait())

    def deliver(i, dy):
        s = i * NY + dy
        return remote(stage2.at[s], recv2.at[s], s2.at[s], r2.at[s], (chip_at(i, dy, 1) * 2 + core, x))

    def pick(i, dy):
        s = i * NY + dy
        there = chip_at(i, dy, 1)
        mine = isinstance(i, int) and i == 0 and dy == 0
        for p in range(CTX_PAGES):
            tile = frag[tabs[p % 8, there * NX + p // 8]]
            if mine:
                recv2[0, p] = tile
            else:
                stage2[s, p] = tile
        if not mine:
            deliver(i, dy).start()

    each(False, pick)
    pick(0, 0)

    start = start_ref[0]
    keys = CTX_PAGES * ROWS
    at = lax.broadcasted_iota(jnp.int32, (1, keys), 1)

    def attend(i):
        base = ((z - dz_of(i) + NZ) % NZ) * ROWS
        allowed = at // ROWS * PAGE + at % ROWS + base < start
        for h in range(KV_HEADS):
            k_slot = i * NY + (y - 2 * h + NY) % NY
            v_slot = i * NY + (y - 2 * h - 1 + NY) % NY
            k = recv2[k_slot].reshape(keys, HEAD)
            v = recv2[v_slot].reshape(keys, HEAD)

            @pl.loop(0, GROUP)
            def _(g):
                n = h * GROUP + g
                q = q_ref[:, pl.ds(pl.multiple_of(n * HEAD, HEAD), HEAD)]
                s = jnp.where(allowed, scores(q, k), -jnp.inf)
                parts = [s[:, j * HEAD:(j + 1) * HEAD] for j in range(keys // HEAD)]
                m_old = m_ref[n]
                m = jnp.maximum(m_old, jnp.max(functools.reduce(jnp.maximum, parts), axis=1, keepdims=True))
                alpha = jnp.exp2(m_old - m)
                ps = [jnp.exp2(part - m) for part in parts]
                m_ref[n] = m
                l_ref[n] = l_ref[n] * alpha + functools.reduce(jnp.add, ps)
                p = jnp.concatenate([part.astype(jnp.bfloat16) for part in ps], axis=1)
                acc_ref[n] = acc_ref[n] * alpha + jnp.dot(p, v, preferred_element_type=jnp.float32)

    for dy in range(1, NY):
        deliver(0, dy).wait_recv()
    attend(0)

    @pl.loop(1, NZ)
    def _(i):
        for dy in range(NY):
            deliver(i, dy).wait_recv()
        attend(i)

    for n in range(KV_HEADS * GROUP):
        total = jnp.sum(l_ref[n], axis=1, keepdims=True)
        out_ref[:, n * HEAD:(n + 1) * HEAD] = (acc_ref[n] / total).astype(jnp.bfloat16)

    each(False, lambda i, dy: spread(i, dy).wait_send())
    each(False, lambda i, dy: deliver(i, dy).wait_send())


ROUNDS = 4
OPEN = 1
PLANE = 2 * NY * SLOTS
WIDTH = (84, 70, 54, 24)
OFF = (0, 128, 198, 252)
TOTAL = OFF[-1] + WIDTH[-1]
JOINED = PLANE + 2 * TOTAL
HOPS = len(WIDTH)
STEP = (1, -1)


def width(r, t):
    return PLANE if t == 1 and r < OPEN else WIDTH[t - 1]


def step_of(n, most):
    return max(d for d in range(1, most + 1) if n % d == 0)


def base_of(s, t):
    return PLANE + s * TOTAL + OFF[t - 1]


def narrow_kernel(
    start_ref, lender_ref, slot_ref, q_any, nk_any, nv_any, pool_ref, out_ref, over_ref,
    q_ref, nk_ref, nv_ref, stage, home, arrive, sbuf, join, ybuf, recv,
    tabx, tabz, tabp, tabv, tabs, need, member, before, place, mat, metav, meta, plist, m_ref, l_ref, acc_ref,
    in_sem, load_sem, own_sem, smem_sem, ms, mr, xs, xr, zs, zr, ps, pr, hs, hr, rs, rr, ys, yr,
):
    inst, x = lax.axis_index("inst"), lax.axis_index("tp")
    core, chip = inst % 2, inst // 2
    z, y = chip % NZ, chip // NZ
    i32 = jnp.int32

    def device(dy, dz, dc):
        return ((((y + dy) % NY) * NZ + (z + dz + NZ) % NZ) * 2 + (core + dc) % 2, x)

    def remote(src, dst, ss, rs_, dev):
        return pltpu.make_async_remote_copy(
            src_ref=src, dst_ref=dst, send_sem=ss, recv_sem=rs_, device_id=dev, device_id_type=MESH
        )

    inputs = [
        pltpu.make_async_copy(src, dst, in_sem.at[n])
        for n, (src, dst) in enumerate(((q_any, q_ref), (nk_any, nk_ref), (nv_any, nv_ref)))
    ]
    def load_all(r):
        for yy in range(NY):
            for half in range(2):
                pltpu.make_async_copy(
                    pool_ref.at[:, yy % 2, pl.ds((2 * r + half) * ROWS, ROWS), pl.ds((yy // 2) * HEAD, HEAD)],
                    stage[r].at[yy, half], load_sem.at[r],
                ).start()

    def loaded(r):
        pltpu.make_async_copy(stage[r], stage[r], load_sem.at[r]).wait()

    load_all(0)

    barrier = pltpu.get_barrier_semaphore()

    def greet(dev):
        pl.semaphore_signal(barrier, inc=1, device_id=dev, device_id_type=MESH)

    for d in range(1, NX):
        greet((inst, (x + d) % NX))

    @pl.loop(1, NZ)
    def _(d):
        greet(device(0, d, 0))

    @pl.loop(1, 2 * NY)
    def _(k):
        greet(device(k // 2, 0, k % 2))

    pl.semaphore_wait(barrier, NX - 1 + NZ - 1 + 2 * NY - 1)

    row = lax.broadcasted_iota(i32, (8, 128), 0)
    lane = lax.broadcasted_iota(i32, (8, 128), 1)
    wanted = (lane == chip * NX + x) & ((x * 8 + row) * PAGE < start_ref[0])
    named = jnp.zeros((8, 128), i32)
    for e in range(8):
        lender = lender_ref[e, 0]
        page = (lender // 2 % NZ) * PLANE + (lender // (2 * NZ) * 2 + lender % 2) * SLOTS + slot_ref[e]
        named = jnp.where(row == e, page + 1, named)
    tabx[0] = jnp.where(wanted, named, 0)

    def table_x(d):
        return remote(tabx.at[0], tabx.at[d], xs.at[d], xr.at[d], (inst, (x + d) % NX))

    for d in range(1, NX):
        table_x(d).start()

    here = pl.ds((y * 2 + core) * SLOTS, SLOTS)

    def spread(r, k):
        dy, dc = k // 2, k % 2
        return remote(
            stage[r].at[(y + dy) % NY, (core + dc) % 2], home[r].at[here], hs.at[r, k], hr.at[r, k], device(dy, 0, dc)
        )

    def own(r):
        return pltpu.make_async_copy(stage[r].at[y, core], home[r].at[here], own_sem.at[r])

    def spread_all(r):
        own(r).start()

        @pl.loop(1, 2 * NY)
        def _(k):
            spread(r, k).start()

    def hop(r, s, t):
        src = home[r] if width(r, t) == PLANE else sbuf.at[r, s, pl.ds(OFF[t - 1], WIDTH[t - 1])]
        return remote(src, arrive[r][s][t - 1], rs.at[r, s, t - 1], rr.at[r, s, t - 1], device(0, STEP[s], 0))

    def piece(s, k):
        part = pl.ds(((y - k // 2 + NY) % NY * 2 + (core + k % 2) % 2) * SLOTS, SLOTS)
        return remote(
            home[0].at[part], arrive[0][s][0].at[part], ms.at[s, k], mr.at[s, k], device(0, STEP[s], 0)
        )

    def send_piece(k):
        if k == 0:
            own(0).wait()
        else:
            spread(0, k).wait_recv()
        for s in range(2):
            piece(s, k).start()

    def wait_hop(r, s, t):
        if r == 0 and t == 1:

            @pl.loop(0, 2 * NY)
            def _(k):
                piece(s, k).wait_recv()

        else:
            hop(r, s, t).wait_recv()

    def ring(r, t):
        if t == 1:
            own(r).wait()

            @pl.loop(1, 2 * NY)
            def _(k):
                spread(r, k).wait_recv()

        lists = 3 if r < OPEN else 1
        for s in range(2):
            source = home[r]
            if t > 1:
                wait_hop(r, s, t - 1)
                source = arrive[r][s][t - 2]
            if width(r, t) < PLANE:

                some = step_of(WIDTH[t - 1], 8)

                @pl.loop(0, WIDTH[t - 1] // some)
                def _(kk):
                    for u in range(some):
                        k = kk * some + u
                        sbuf[r, s, OFF[t - 1] + k] = source[meta[lists, s * HOPS + t - 1, k]]

            hop(r, s, t).start()

    loaded(0)
    spread_all(0)
    send_piece(0)
    for d in range(1, NX):
        table_x(d).wait()
    tabz[0] = tabx[0] + tabx[1] + tabx[2] + tabx[3]

    def table_z(d):
        return remote(tabz.at[0], tabz.at[d], zs.at[d], zr.at[d], device(0, d, 0))

    @pl.loop(1, NZ)
    def _(d):
        table_z(d).start()

    send_piece(1)
    for r in range(1, ROUNDS):
        load_all(r)
    for copy in inputs:
        copy.start()
    for k in (2, 6, 3, 7):
        send_piece(k)

    @pl.loop(1, NZ)
    def _(d):
        table_z(d).wait()

    tabp[0] = functools.reduce(jnp.add, [tabz[d] for d in range(NZ)])

    def table_p(k):
        return remote(tabp.at[0], tabp.at[k], ps.at[k], pr.at[k], device(k // 2, 0, k % 2))

    @pl.loop(1, 2 * NY)
    def _(k):
        table_p(k).start()

    loaded(1)
    spread_all(1)
    for k in (4, 5):
        send_piece(k)

    def new_tokens():
        for copy in inputs:
            copy.wait()
        rows_ = lax.broadcasted_iota(i32, (GROUP * PAGE, PAGE), 0) % PAGE
        cols_ = lax.broadcasted_iota(i32, (GROUP * PAGE, PAGE), 1)

        @pl.loop(0, KV_HEADS)
        def _(h):
            head = pl.ds(pl.multiple_of(h * HEAD, HEAD), HEAD)
            n = pl.ds(h * GROUP, GROUP)
            q = jnp.concatenate(
                [q_ref[:, pl.ds(pl.multiple_of((h * GROUP + e) * HEAD, HEAD), HEAD)] for e in range(GROUP)], axis=0
            )
            s = jnp.where(cols_ <= rows_, scores(q, nk_ref[:, head]), -jnp.inf)
            m = jnp.broadcast_to(jnp.max(s, axis=1, keepdims=True), s.shape)
            p = jnp.exp2(s - m)
            m_ref[n] = m.reshape(GROUP, PAGE, HEAD)
            l_ref[n] = p.reshape(GROUP, PAGE, HEAD)
            acc = jnp.dot(p.astype(jnp.bfloat16), nv_ref[:, head], preferred_element_type=jnp.float32)
            acc_ref[n] = acc.reshape(GROUP, PAGE, HEAD)

    new_tokens()

    @pl.loop(1, 2 * NY)
    def _(k):
        table_p(k).wait()

    for dc in range(2):
        tabv[dc] = functools.reduce(jnp.add, [tabp[2 * dy + dc] for dy in range(NY)])
    to_smem = pltpu.make_async_copy(tabv, tabs, smem_sem.at[0])
    to_smem.start()
    to_smem.wait()

    number = row * PLANE + lane + 1

    @pl.loop(0, NZ)
    def _(d):
        hit = jnp.zeros((8, 128), i32)
        for dc in range(2):
            for yy in range(NY):
                for xx in range(NX):
                    for e in range(8):
                        hit = jnp.where(number == tabs[dc, e, (yy * NZ + d) * NX + xx], 1, hit)
        need[d] = hit

    if OPEN > 1:
        ring(1, 1)

    def ahead(k):
        return functools.reduce(jnp.add, [jnp.where(row == (d - k) % NZ, need[d], 0) for d in range(NZ)])

    even = lane % 2 == 0
    far = ahead(NZ // 2)
    over = None
    for s in range(2):
        users = [jnp.where(even if s == 0 else ~even, far, 0)]
        for t in range(HOPS - 1, 0, -1):
            users.insert(0, users[0] | ahead(t if s == 0 else NZ - t))
        for t in range(1, HOPS + 1):
            n = s * HOPS + t - 1
            count = users[t - 1]
            shift = 1
            while shift < 128:
                count = count + jnp.where(lane >= shift, pltpu.roll(count, shift, 1), 0)
                shift *= 2
            excess = count - WIDTH[t - 1]
            over = excess if over is None else jnp.maximum(over, excess)
            count = count - users[t - 1]
            member[n] = users[t - 1]
            before[n] = count
            place[n] = jnp.minimum(count, WIDTH[t - 1] - 1)
    over_ref[0, 0] = jnp.max(over)

    for variant in range(2):
        where_to = jnp.where(row == z, lane, 0)
        for s in range(2):
            for t in range(1, HOPS + 1):
                mine = row == (z - STEP[s] * t + NZ) % NZ
                if t == HOPS:
                    mine = mine & (even if s == 0 else ~even)
                at_hop = lane if variant and t == 1 else place[s * HOPS + t - 1]
                where_to = where_to + jnp.where(mine, base_of(s, t) + at_hop, 0)
        metav[2 * variant] = where_to

    mat[...] = jnp.zeros_like(mat)
    for s in range(2):
        for t in range(1, HOPS + 1):
            n = s * HOPS + t - 1
            o = pl.ds((z - STEP[s] * (t - 1) + NZ) % NZ, 1)
            mat[n:n + 1] = jnp.where(member[n, o] > 0, before[n, o], 999)
            mat[8 + n:9 + n] = lane[0:1] if t == 1 else place[n - 1, o]
    turned = mat[...].T
    lanes = lax.broadcasted_iota(i32, (128, 128), 1)
    pages = lax.broadcasted_iota(i32, (128, 128), 0)
    for n in range(2 * HOPS):
        goes = turned[:, n:n + 1] == lanes
        row_n = jnp.sum(jnp.where(goes, turned[:, 8 + n:9 + n], 0), axis=0, keepdims=True)
        metav[1, n:n + 1] = row_n
        if n % HOPS == 1:
            row_n = jnp.sum(jnp.where(goes, pages, 0), axis=0, keepdims=True)
        metav[3, n:n + 1] = row_n
    to_smem2 = pltpu.make_async_copy(metav, meta, smem_sem.at[1])
    to_smem2.start()
    to_smem2.wait()

    def find():
        @pl.loop(0, 2 * NY)
        def _(k):
            column = (((y + k // 2) % NY) * NZ + z) * NX
            for p in range(CTX_PAGES):
                e = jnp.maximum(tabs[k % 2, p % 8, column + p // 8] - 1, 0)
                for variant in range(2):
                    plist[variant * 2 * NY + k, p] = meta[2 * variant, e // PLANE, e % PLANE]

    def deliver(r, k):
        return remote(ybuf.at[r, k], recv.at[r, k], ys.at[r, k], yr.at[r, k], device(k // 2, 0, k % 2))

    def hand_out(r):
        def gather(s, t):
            some = step_of(width(r, t), 16)

            @pl.loop(0, width(r, t) // some)
            def _(j):
                join[pl.ds(base_of(s, t) + j * some, some)] = arrive[r][s][t - 1][pl.ds(j * some, some)]

        @pl.loop(0, PLANE // 8)
        def _(j):
            join[pl.ds(j * 8, 8)] = home[r][pl.ds(j * 8, 8)]

        for t in range(1, HOPS + 1):
            for s in range(2):
                if t == HOPS:
                    hop(r, s, HOPS).wait_recv()
                gather(s, t)

        lists = 2 * NY if r < OPEN else 0

        def pick(k):
            for p in range(CTX_PAGES):
                ybuf[r, k, p] = join[plist[lists + k, p]]
            deliver(r, k).start()

        @pl.loop(1, NY)
        def _(dy):
            pick(2 * dy)

        @pl.loop(0, NY)
        def _(dy):
            pick(2 * dy + 1)

        for p in range(CTX_PAGES):
            recv[r, 0, p] = join[plist[lists, p]]

    start = start_ref[0]
    keys = CTX_PAGES * ROWS
    at = lax.broadcasted_iota(i32, (1, keys), 1)

    def attend(r, dc, h):
        tb = 2 * r + (core + dc) % 2
        allowed = at // ROWS * PAGE + at % ROWS + tb * ROWS < start
        k = recv[r, (y - 2 * h + NY) % NY * 2 + dc].reshape(keys, HEAD)
        v = recv[r, (y - 2 * h - 1 + NY) % NY * 2 + dc].reshape(keys, HEAD)

        @pl.loop(0, GROUP // PAIR, unroll=UNROLL)
        def _(g):
            n = h * GROUP + g * PAIR
            wide_row = (PAIR * PAGE, HEAD)
            q = jnp.concatenate(
                [q_ref[:, pl.ds(pl.multiple_of((n + e) * HEAD, HEAD), HEAD)] for e in range(PAIR)], axis=0
            )
            s = jnp.where(allowed, scores(q, k), -jnp.inf)
            parts = [s[:, j * HEAD:(j + 1) * HEAD] for j in range(keys // HEAD)]
            m_old = m_ref[pl.ds(n, PAIR)].reshape(wide_row)
            m = jnp.maximum(m_old, jnp.max(functools.reduce(jnp.maximum, parts), axis=1, keepdims=True))
            alpha = jnp.exp2(m_old - m)
            ps_ = [jnp.exp2(part - m) for part in parts]
            m_ref[pl.ds(n, PAIR)] = m.reshape(PAIR, PAGE, HEAD)
            l = l_ref[pl.ds(n, PAIR)].reshape(wide_row) * alpha + functools.reduce(jnp.add, ps_)
            l_ref[pl.ds(n, PAIR)] = l.reshape(PAIR, PAGE, HEAD)
            p = jnp.concatenate([part.astype(jnp.bfloat16) for part in ps_], axis=1)
            acc = acc_ref[pl.ds(n, PAIR)].reshape(wide_row) * alpha
            acc = acc + jnp.dot(p, v, preferred_element_type=jnp.float32)
            acc_ref[pl.ds(n, PAIR)] = acc.reshape(PAIR, PAGE, HEAD)

    def units(r, first, last):
        for dc in range(2):
            if first <= 2 * dc < last:

                @pl.loop(1 - dc, NY)
                def _(dy):
                    deliver(r, 2 * dy + dc).wait_recv()

            lo, hi = max(first, 2 * dc), min(last, 2 * dc + 2)
            if lo < hi:

                @pl.loop(lo - 2 * dc, hi - 2 * dc)
                def _(h):
                    attend(r, dc, h)

    if OPEN == 1:
        ring(1, 1)
    for r in range(2, ROUNDS):
        loaded(r)
        spread_all(r)
    ring(0, 2)
    ring(2, 1)
    find()
    ring(0, 3)
    ring(1, 2)
    ring(3, 1)
    ring(0, 4)
    ring(1, 3)
    ring(2, 2)
    hand_out(0)
    ring(1, 4)
    ring(2, 3)
    units(0, 0, 2)
    hand_out(1)
    ring(3, 2)
    units(0, 2, 4)
    ring(2, 4)
    units(1, 0, 1)
    ring(3, 3)
    units(1, 1, 2)
    hand_out(2)
    ring(3, 4)
    units(1, 2, 4)
    hand_out(3)
    units(2, 0, 4)
    units(3, 0, 4)

    for n in range(KV_HEADS * GROUP):
        total = jnp.sum(l_ref[n], axis=1, keepdims=True)
        out_ref[:, n * HEAD:(n + 1) * HEAD] = (acc_ref[n] * (1.0 / total)).astype(jnp.bfloat16)

    for r in range(ROUNDS):

        @pl.loop(1, 2 * NY)
        def _(k):
            spread(r, k).wait_send()
            deliver(r, k).wait_send()

        for s in range(2):
            for t in range(1, HOPS + 1):
                if r == 0 and t == 1:

                    @pl.loop(0, 2 * NY)
                    def _(k):
                        piece(s, k).wait_send()

                else:
                    hop(r, s, t).wait_send()


def narrow(queries, new_keys, fresh_values, lent_page_pool, page_lender, page_slot, starts):
    vmem, smem, hbm = (pl.BlockSpec(memory_space=space) for space in (pltpu.VMEM, pltpu.SMEM, pl.ANY))
    dma = pltpu.SemaphoreType.DMA
    heads = KV_HEADS * GROUP
    bf16, f32, i32 = jnp.bfloat16, jnp.float32, jnp.int32
    tiles = lambda *n: pltpu.VMEM((*n, ROWS, HEAD), bf16)
    ints = lambda *n: pltpu.VMEM((*n, 8, 128), i32)
    return pl.pallas_call(
        narrow_kernel,
        out_shape=(jax.ShapeDtypeStruct(queries.shape, bf16), jax.ShapeDtypeStruct((1, 1), i32)),
        in_specs=[smem, smem, smem, hbm, hbm, hbm, hbm],
        out_specs=(vmem, smem),
        scratch_shapes=[
            pltpu.VMEM(queries.shape, bf16), pltpu.VMEM(new_keys.shape, bf16), pltpu.VMEM(fresh_values.shape, bf16),
            [tiles(NY, 2, SLOTS) for _ in range(ROUNDS)],
            [tiles(PLANE) for _ in range(ROUNDS)],
            [[[tiles(width(r, t + 1)) for t in range(HOPS)] for _ in range(2)] for r in range(ROUNDS)],
            tiles(ROUNDS, 2, TOTAL), tiles(JOINED),
            tiles(ROUNDS, 2 * NY, CTX_PAGES), tiles(ROUNDS, 2 * NY, CTX_PAGES),
            ints(NX), ints(NZ), ints(2 * NY), ints(2), pltpu.SMEM((2, 8, 128), i32),
            ints(NZ), ints(2 * HOPS), ints(2 * HOPS), ints(2 * HOPS), pltpu.VMEM((128, 128), i32),
            ints(4), pltpu.SMEM((4, 8, 128), i32), pltpu.SMEM((16, 128), i32),
            pltpu.VMEM((heads, PAGE, HEAD), f32), pltpu.VMEM((heads, PAGE, HEAD), f32), pltpu.VMEM((heads, PAGE, HEAD), f32),
            dma((3,)), dma((ROUNDS,)), dma((ROUNDS,)), dma((2,)), dma((2, 2 * NY)), dma((2, 2 * NY)),
            dma((NX,)), dma((NX,)), dma((NZ,)), dma((NZ,)), dma((2 * NY,)), dma((2 * NY,)),
            dma((ROUNDS, 2 * NY)), dma((ROUNDS, 2 * NY)),
            dma((ROUNDS, 2, HOPS)), dma((ROUNDS, 2, HOPS)),
            dma((ROUNDS, 2 * NY)), dma((ROUNDS, 2 * NY)),
        ],
        compiler_params=pltpu.CompilerParams(
            collective_id=1, has_side_effects=True, vmem_limit_bytes=56 * 1024 * 1024
        ),
        cost_estimate=pl.CostEstimate(
            flops=4 * heads * PAGE * HEAD * (CTX_PAGES + 1) * PAGE,
            bytes_accessed=4 << 20,
            transcendentals=heads * PAGE * (CTX_PAGES + 1) * PAGE,
        ),
    )(starts, page_lender, page_slot, queries, new_keys, fresh_values, lent_page_pool)


def wide(queries, new_keys, fresh_values, lent_page_pool, page_lender, page_slot, starts):
    pages = page_lender * SLOTS + page_slot[:, None]
    table = jnp.broadcast_to(pages, (8, 128))
    vmem = pl.BlockSpec(memory_space=pltpu.VMEM)
    dma = pltpu.SemaphoreType.DMA
    heads = KV_HEADS * GROUP
    bf16, f32, i32 = jnp.bfloat16, jnp.float32, jnp.int32
    return pl.pallas_call(
        wide_kernel,
        out_shape=jax.ShapeDtypeStruct(queries.shape, bf16),
        in_specs=[
            pl.BlockSpec(memory_space=pltpu.SMEM), vmem, vmem, vmem, pl.BlockSpec(memory_space=pl.ANY), vmem,
        ],
        out_specs=vmem,
        scratch_shapes=[
            pltpu.VMEM((CHIPS, SLOTS, ROWS, HEAD), bf16),
            pltpu.VMEM((CHIPS * 2 * SLOTS, ROWS, HEAD), bf16),
            pltpu.VMEM((CHIPS, CTX_PAGES, ROWS, HEAD), bf16),
            pltpu.VMEM((CHIPS, CTX_PAGES, ROWS, HEAD), bf16),
            pltpu.VMEM((NX, 8, 128), i32),
            pltpu.VMEM((CHIPS, 8, 128), i32),
            pltpu.VMEM((8, 128), i32),
            pltpu.SMEM((8, 128), i32),
            pltpu.VMEM((heads, PAGE, HEAD), f32),
            pltpu.VMEM((heads, PAGE, HEAD), f32),
            pltpu.VMEM((heads, PAGE, HEAD), f32),
            dma, dma, dma,
            dma((NX,)), dma((NX,)),
            dma((CHIPS,)), dma((CHIPS,)),
            dma((CHIPS,)), dma((CHIPS,)),
            dma((CHIPS,)), dma((CHIPS,)),
            dma((CHIPS,)), dma((CHIPS,)),
        ],
        compiler_params=pltpu.CompilerParams(
            collective_id=0, has_side_effects=True, vmem_limit_bytes=48 * 1024 * 1024
        ),
        cost_estimate=pl.CostEstimate(
            flops=4 * heads * PAGE * HEAD * (CTX_PAGES + 1) * PAGE,
            bytes_accessed=4 << 20,
            transcendentals=heads * PAGE * (CTX_PAGES + 1) * PAGE,
        ),
    )(starts, queries, new_keys, fresh_values, lent_page_pool, table)


def local(*args):
    out, over = narrow(*args)
    return lax.cond(over[0, 0] > 0, lambda: wide(*args), lambda: out)


def solution(mesh):
    in_specs = (
        P("inst", "tp"),
        P("inst", "tp"),
        P("inst", "tp"),
        P("inst", None, None, "tp"),
        P(("inst", "tp"), None),
        P(("inst", "tp")),
        P("inst"),
    )
    return jax.shard_map(local, mesh=mesh, in_specs=in_specs, out_specs=P("inst", "tp"), check_vma=False)
```

```python
import functools
import math

import jax
import jax.numpy as jnp
from jax import lax
from jax.experimental import pallas as pl
from jax.experimental.pallas import tpu as pltpu
from jax.sharding import PartitionSpec as P

MESH = pl.DeviceIdType.MESH
HEAD = 128
PAGE = 128
NY, NZ, NX = 4, 8, 4
CHIPS = NY * NZ
SLOTS = 16
CTX_PAGES = 32
ROWS = PAGE // NZ
GROUP = 8
KV_HEADS = 2
UNROLL = 1
PAIR = 8
SCALE = math.log2(math.e) / math.sqrt(HEAD)


def dz_of(i):
    return (i % 2) * ((i + 1) // 2) + (1 - i % 2) * ((NZ - i // 2) % NZ)


def scores(q, k):
    return lax.dot_general(q, k, (((1,), (1,)), ((), ())), preferred_element_type=jnp.float32) * SCALE


def wide_kernel(
    start_ref, q_ref, nk_ref, nv_ref, pool_ref, tab_ref, out_ref,
    stage1, frag, stage2, recv2, tabx, tabj, tabsum, tabs, m_ref, l_ref, acc_ref,
    load_sem, own_sem, smem_sem, xs, xr, ts, tr, s1, r1, fs, fr, s2, r2,
):
    inst, x = lax.axis_index("inst"), lax.axis_index("tp")
    core, chip = inst % 2, inst // 2
    z, y = chip % NZ, chip // NZ
    sibling = (chip * 2 + 1 - core, x)

    def chip_at(i, dy, sign):
        dz = dz_of(i)
        return ((y + sign * dy + NY) % NY) * NZ + (z + sign * dz + NZ) % NZ

    def remote(src, dst, ss, rs, device):
        return pltpu.make_async_remote_copy(
            src_ref=src, dst_ref=dst, send_sem=ss, recv_sem=rs, device_id=device, device_id_type=MESH
        )

    def each(first, body):
        for dy in range(0 if first else 1, NY):
            body(0, dy)

        @pl.loop(1, NZ)
        def _(i):
            for dy in range(NY):
                body(i, dy)

    def load(t):
        yy, zz = t // NZ, t % NZ
        return pltpu.make_async_copy(
            pool_ref.at[:, yy % 2, pl.ds(zz * ROWS, ROWS), pl.ds((yy // 2) * HEAD, HEAD)], stage1.at[t], load_sem
        )

    for t in range(CHIPS):
        load(t).start()

    barrier = pltpu.get_barrier_semaphore()

    def greet(i, dy):
        pl.semaphore_signal(barrier, inc=1, device_id=(chip_at(i, dy, 1) * 2 + core, x), device_id_type=MESH)

    each(False, greet)
    pl.semaphore_signal(barrier, inc=1, device_id=sibling, device_id_type=MESH)
    for d in range(1, NX):
        pl.semaphore_signal(barrier, inc=1, device_id=(inst, (x + d) % NX), device_id_type=MESH)
    pl.semaphore_wait(barrier, CHIPS - 1 + 1 + NX - 1)

    lane = lax.broadcasted_iota(jnp.int32, (8, 128), 1)
    tabx[0] = jnp.where(lane == chip * NX + x, tab_ref[...], 0)

    def table_x(d):
        return remote(tabx.at[0], tabx.at[d], xs.at[d], xr.at[d], (inst, (x + d) % NX))

    for d in range(1, NX):
        table_x(d).start()

    pltpu.make_async_copy(stage1, stage1, load_sem).wait()

    def spread(i, dy):
        t = chip_at(i, dy, 1)
        return remote(
            stage1.at[t], frag.at[pl.ds(inst * SLOTS, SLOTS)], s1.at[i * NY + dy], r1.at[i * NY + dy], (t * 2 + core, x)
        )

    each(False, lambda i, dy: spread(i, dy).start())
    own = pltpu.make_async_copy(stage1.at[chip], frag.at[pl.ds(inst * SLOTS, SLOTS)], own_sem)
    own.start()

    for d in range(1, NX):
        table_x(d).wait()
    tabj[0] = tabx[0] + tabx[1] + tabx[2] + tabx[3]

    def table_j(i, dy):
        s = i * NY + dy
        return remote(tabj.at[0], tabj.at[s], ts.at[s], tr.at[s], (chip_at(i, dy, 1) * 2 + core, x))

    each(False, lambda i, dy: table_j(i, dy).start())

    row = lax.broadcasted_iota(jnp.int32, (PAGE, PAGE), 0)
    col = lax.broadcasted_iota(jnp.int32, (PAGE, PAGE), 1)
    for h in range(KV_HEADS):
        heads = pl.ds(h * HEAD, HEAD)

        @pl.loop(0, GROUP)
        def _(g):
            n = h * GROUP + g
            q = q_ref[:, pl.ds(pl.multiple_of(n * HEAD, HEAD), HEAD)]
            s = jnp.where(col <= row, scores(q, nk_ref[:, heads]), -jnp.inf)
            m = jnp.broadcast_to(jnp.max(s, axis=1, keepdims=True), s.shape)
            p = jnp.exp2(s - m)
            m_ref[n] = m
            l_ref[n] = p
            acc_ref[n] = jnp.dot(p.astype(jnp.bfloat16), nv_ref[:, heads], preferred_element_type=jnp.float32)

    own.wait()

    def forward(i, dy):
        lender = chip_at(i, dy, -1) * 2 + core
        part = frag.at[pl.ds(lender * SLOTS, SLOTS)]
        return remote(part, part, fs.at[i * NY + dy], fr.at[i * NY + dy], sibling)

    def pass_on(i, dy):
        if not (isinstance(i, int) and i == 0 and dy == 0):
            spread(i, dy).wait_recv()
        forward(i, dy).start()

    each(True, pass_on)

    each(False, lambda i, dy: table_j(i, dy).wait())
    total = tabj[0]
    for s in range(1, CHIPS):
        total = total + tabj[s]
    tabsum[...] = total
    to_smem = pltpu.make_async_copy(tabsum, tabs, smem_sem)
    to_smem.start()
    to_smem.wait()

    each(True, lambda i, dy: forward(i, dy).wait())

    def deliver(i, dy):
        s = i * NY + dy
        return remote(stage2.at[s], recv2.at[s], s2.at[s], r2.at[s], (chip_at(i, dy, 1) * 2 + core, x))

    def pick(i, dy):
        s = i * NY + dy
        there = chip_at(i, dy, 1)
        mine = isinstance(i, int) and i == 0 and dy == 0
        for p in range(CTX_PAGES):
            tile = frag[tabs[p % 8, there * NX + p // 8]]
            if mine:
                recv2[0, p] = tile
            else:
                stage2[s, p] = tile
        if not mine:
            deliver(i, dy).start()

    each(False, pick)
    pick(0, 0)

    start = start_ref[0]
    keys = CTX_PAGES * ROWS
    at = lax.broadcasted_iota(jnp.int32, (1, keys), 1)

    def attend(i):
        base = ((z - dz_of(i) + NZ) % NZ) * ROWS
        allowed = at // ROWS * PAGE + at % ROWS + base < start
        for h in range(KV_HEADS):
            k_slot = i * NY + (y - 2 * h + NY) % NY
            v_slot = i * NY + (y - 2 * h - 1 + NY) % NY
            k = recv2[k_slot].reshape(keys, HEAD)
            v = recv2[v_slot].reshape(keys, HEAD)

            @pl.loop(0, GROUP)
            def _(g):
                n = h * GROUP + g
                q = q_ref[:, pl.ds(pl.multiple_of(n * HEAD, HEAD), HEAD)]
                s = jnp.where(allowed, scores(q, k), -jnp.inf)
                parts = [s[:, j * HEAD:(j + 1) * HEAD] for j in range(keys // HEAD)]
                m_old = m_ref[n]
                m = jnp.maximum(m_old, jnp.max(functools.reduce(jnp.maximum, parts), axis=1, keepdims=True))
                alpha = jnp.exp2(m_old - m)
                ps = [jnp.exp2(part - m) for part in parts]
                m_ref[n] = m
                l_ref[n] = l_ref[n] * alpha + functools.reduce(jnp.add, ps)
                p = jnp.concatenate([part.astype(jnp.bfloat16) for part in ps], axis=1)
                acc_ref[n] = acc_ref[n] * alpha + jnp.dot(p, v, preferred_element_type=jnp.float32)

    for dy in range(1, NY):
        deliver(0, dy).wait_recv()
    attend(0)

    @pl.loop(1, NZ)
    def _(i):
        for dy in range(NY):
            deliver(i, dy).wait_recv()
        attend(i)

    for n in range(KV_HEADS * GROUP):
        total = jnp.sum(l_ref[n], axis=1, keepdims=True)
        out_ref[:, n * HEAD:(n + 1) * HEAD] = (acc_ref[n] / total).astype(jnp.bfloat16)

    each(False, lambda i, dy: spread(i, dy).wait_send())
    each(False, lambda i, dy: deliver(i, dy).wait_send())


ROUNDS = 4
OPEN = 1
PLANE = 2 * NY * SLOTS
WIDTH = (84, 70, 54, 24)
OFF = (0, 128, 198, 252)
TOTAL = OFF[-1] + WIDTH[-1]
JOINED = PLANE + 2 * TOTAL
HOPS = len(WIDTH)
STEP = (1, -1)


def width(r, t):
    return PLANE if t == 1 and r < OPEN else WIDTH[t - 1]


def step_of(n, most):
    return max(d for d in range(1, most + 1) if n % d == 0)


def base_of(s, t):
    return PLANE + s * TOTAL + OFF[t - 1]


def narrow_kernel(
    start_ref, lender_ref, slot_ref, q_any, nk_any, nv_any, pool_ref, out_ref, over_ref,
    q_ref, nk_ref, nv_ref, stage, home, arrive, sbuf, join, ybuf, recv,
    tabx, tabz, tabp, tabv, tabs, need, member, before, place, mat, metav, meta, plist, m_ref, l_ref, acc_ref,
    in_sem, load_sem, own_sem, smem_sem, ms, mr, xs, xr, zs, zr, ps, pr, hs, hr, rs, rr, ys, yr,
):
    inst, x = lax.axis_index("inst"), lax.axis_index("tp")
    core, chip = inst % 2, inst // 2
    z, y = chip % NZ, chip // NZ
    i32 = jnp.int32

    def device(dy, dz, dc):
        return ((((y + dy) % NY) * NZ + (z + dz + NZ) % NZ) * 2 + (core + dc) % 2, x)

    def remote(src, dst, ss, rs_, dev):
        return pltpu.make_async_remote_copy(
            src_ref=src, dst_ref=dst, send_sem=ss, recv_sem=rs_, device_id=dev, device_id_type=MESH
        )

    inputs = [
        pltpu.make_async_copy(src, dst, in_sem.at[n])
        for n, (src, dst) in enumerate(((q_any, q_ref), (nk_any, nk_ref), (nv_any, nv_ref)))
    ]
    def load_all(r):
        for yy in range(NY):
            for half in range(2):
                pltpu.make_async_copy(
                    pool_ref.at[:, yy % 2, pl.ds((2 * r + half) * ROWS, ROWS), pl.ds((yy // 2) * HEAD, HEAD)],
                    stage[r].at[yy, half], load_sem.at[r],
                ).start()

    def loaded(r):
        pltpu.make_async_copy(stage[r], stage[r], load_sem.at[r]).wait()

    barrier = pltpu.get_barrier_semaphore()

    def greet(dev):
        pl.semaphore_signal(barrier, inc=1, device_id=dev, device_id_type=MESH)

    for d in range(1, NX):
        greet((inst, (x + d) % NX))

    @pl.loop(1, NZ)
    def _(d):
        greet(device(0, d, 0))

    @pl.loop(1, 2 * NY)
    def _(k):
        greet(device(k // 2, 0, k % 2))

    load_all(0)

    row = lax.broadcasted_iota(i32, (8, 128), 0)
    lane = lax.broadcasted_iota(i32, (8, 128), 1)
    wanted = (lane == chip * NX + x) & ((x * 8 + row) * PAGE < start_ref[0])
    named = jnp.zeros((8, 128), i32)
    for e in range(8):
        lender = lender_ref[e, 0]
        page = (lender // 2 % NZ) * PLANE + (lender // (2 * NZ) * 2 + lender % 2) * SLOTS + slot_ref[e]
        named = jnp.where(row == e, page + 1, named)
    tabx[0] = jnp.where(wanted, named, 0)

    pl.semaphore_wait(barrier, NX - 1 + NZ - 1 + 2 * NY - 1)

    def table_x(d):
        return remote(tabx.at[0], tabx.at[d], xs.at[d], xr.at[d], (inst, (x + d) % NX))

    for d in range(1, NX):
        table_x(d).start()

    here = pl.ds((y * 2 + core) * SLOTS, SLOTS)

    def spread(r, k):
        dy, dc = k // 2, k % 2
        return remote(
            stage[r].at[(y + dy) % NY, (core + dc) % 2], home[r].at[here], hs.at[r, k], hr.at[r, k], device(dy, 0, dc)
        )

    def own(r):
        return pltpu.make_async_copy(stage[r].at[y, core], home[r].at[here], own_sem.at[r])

    def spread_all(r):
        own(r).start()

        @pl.loop(1, 2 * NY)
        def _(k):
            spread(r, k).start()

    def hop(r, s, t):
        src = home[r] if width(r, t) == PLANE else sbuf.at[r, s, pl.ds(OFF[t - 1], WIDTH[t - 1])]
        return remote(src, arrive[r][s][t - 1], rs.at[r, s, t - 1], rr.at[r, s, t - 1], device(0, STEP[s], 0))

    def piece(s, k):
        part = pl.ds(((y - k // 2 + NY) % NY * 2 + (core + k % 2) % 2) * SLOTS, SLOTS)
        return remote(
            home[0].at[part], arrive[0][s][0].at[part], ms.at[s, k], mr.at[s, k], device(0, STEP[s], 0)
        )

    def send_piece(k):
        if k == 0:
            own(0).wait()
        else:
            spread(0, k).wait_recv()
        for s in range(2):
            piece(s, k).start()

    def wait_hop(r, s, t):
        if r == 0 and t == 1:

            @pl.loop(0, 2 * NY)
            def _(k):
                piece(s, k).wait_recv()

        else:
            hop(r, s, t).wait_recv()

    def ring(r, t):
        if t == 1:
            own(r).wait()

            @pl.loop(1, 2 * NY)
            def _(k):
                spread(r, k).wait_recv()

        lists = 3 if r < OPEN else 1
        for s in range(2):
            source = home[r]
            if t > 1:
                wait_hop(r, s, t - 1)
                source = arrive[r][s][t - 2]
            if width(r, t) < PLANE:

                some = step_of(WIDTH[t - 1], 8)

                @pl.loop(0, WIDTH[t - 1] // some)
                def _(kk):
                    for u in range(some):
                        k = kk * some + u
                        sbuf[r, s, OFF[t - 1] + k] = source[meta[lists, s * HOPS + t - 1, k]]

            hop(r, s, t).start()

    loaded(0)
    spread_all(0)
    send_piece(0)
    for d in range(1, NX):
        table_x(d).wait()
    tabz[0] = tabx[0] + tabx[1] + tabx[2] + tabx[3]

    def table_z(d):
        return remote(tabz.at[0], tabz.at[d], zs.at[d], zr.at[d], device(0, d, 0))

    @pl.loop(1, NZ)
    def _(d):
        table_z(d).start()

    send_piece(1)
    for r in range(1, ROUNDS):
        load_all(r)
    for copy in inputs:
        copy.start()
    for k in (2, 6, 3, 7):
        send_piece(k)

    @pl.loop(1, NZ)
    def _(d):
        table_z(d).wait()

    tabp[0] = functools.reduce(jnp.add, [tabz[d] for d in range(NZ)])

    def table_p(k):
        return remote(tabp.at[0], tabp.at[k], ps.at[k], pr.at[k], device(k // 2, 0, k % 2))

    @pl.loop(1, 2 * NY)
    def _(k):
        table_p(k).start()

    loaded(1)
    spread_all(1)
    for k in (4, 5):
        send_piece(k)

    def new_tokens():
        for copy in inputs:
            copy.wait()
        rows_ = lax.broadcasted_iota(i32, (GROUP * PAGE, PAGE), 0) % PAGE
        cols_ = lax.broadcasted_iota(i32, (GROUP * PAGE, PAGE), 1)

        @pl.loop(0, KV_HEADS)
        def _(h):
            head = pl.ds(pl.multiple_of(h * HEAD, HEAD), HEAD)
            n = pl.ds(h * GROUP, GROUP)
            q = jnp.concatenate(
                [q_ref[:, pl.ds(pl.multiple_of((h * GROUP + e) * HEAD, HEAD), HEAD)] for e in range(GROUP)], axis=0
            )
            s = jnp.where(cols_ <= rows_, scores(q, nk_ref[:, head]), -jnp.inf)
            m = jnp.broadcast_to(jnp.max(s, axis=1, keepdims=True), s.shape)
            p = jnp.exp2(s - m)
            m_ref[n] = m.reshape(GROUP, PAGE, HEAD)
            l_ref[n] = p.reshape(GROUP, PAGE, HEAD)
            acc = jnp.dot(p.astype(jnp.bfloat16), nv_ref[:, head], preferred_element_type=jnp.float32)
            acc_ref[n] = acc.reshape(GROUP, PAGE, HEAD)

    new_tokens()

    @pl.loop(1, 2 * NY)
    def _(k):
        table_p(k).wait()

    for dc in range(2):
        tabv[dc] = functools.reduce(jnp.add, [tabp[2 * dy + dc] for dy in range(NY)])
    to_smem = pltpu.make_async_copy(tabv, tabs, smem_sem.at[0])
    to_smem.start()
    to_smem.wait()

    number = row * PLANE + lane + 1

    @pl.loop(0, NZ)
    def _(d):
        hit = jnp.zeros((8, 128), i32)
        for dc in range(2):
            for yy in range(NY):
                for xx in range(NX):
                    for e in range(8):
                        hit = jnp.where(number == tabs[dc, e, (yy * NZ + d) * NX + xx], 1, hit)
        need[d] = hit

    if OPEN > 1:
        ring(1, 1)

    def ahead(k):
        return functools.reduce(jnp.add, [jnp.where(row == (d - k) % NZ, need[d], 0) for d in range(NZ)])

    even = lane % 2 == 0
    far = ahead(NZ // 2)
    over = None
    for s in range(2):
        users = [jnp.where(even if s == 0 else ~even, far, 0)]
        for t in range(HOPS - 1, 0, -1):
            users.insert(0, users[0] | ahead(t if s == 0 else NZ - t))
        for t in range(1, HOPS + 1):
            n = s * HOPS + t - 1
            count = users[t - 1]
            shift = 1
            while shift < 128:
                count = count + jnp.where(lane >= shift, pltpu.roll(count, shift, 1), 0)
                shift *= 2
            excess = count - WIDTH[t - 1]
            over = excess if over is None else jnp.maximum(over, excess)
            count = count - users[t - 1]
            member[n] = users[t - 1]
            before[n] = count
            place[n] = jnp.minimum(count, WIDTH[t - 1] - 1)
    over_ref[0, 0] = jnp.max(over)

    for variant in range(2):
        where_to = jnp.where(row == z, lane, 0)
        for s in range(2):
            for t in range(1, HOPS + 1):
                mine = row == (z - STEP[s] * t + NZ) % NZ
                if t == HOPS:
                    mine = mine & (even if s == 0 else ~even)
                at_hop = lane if variant and t == 1 else place[s * HOPS + t - 1]
                where_to = where_to + jnp.where(mine, base_of(s, t) + at_hop, 0)
        metav[2 * variant] = where_to

    mat[...] = jnp.zeros_like(mat)
    for s in range(2):
        for t in range(1, HOPS + 1):
            n = s * HOPS + t - 1
            o = pl.ds((z - STEP[s] * (t - 1) + NZ) % NZ, 1)
            mat[n:n + 1] = jnp.where(member[n, o] > 0, before[n, o], 999)
            mat[8 + n:9 + n] = lane[0:1] if t == 1 else place[n - 1, o]
    turned = mat[...].T
    lanes = lax.broadcasted_iota(i32, (128, 128), 1)
    pages = lax.broadcasted_iota(i32, (128, 128), 0)
    for n in range(2 * HOPS):
        goes = turned[:, n:n + 1] == lanes
        row_n = jnp.sum(jnp.where(goes, turned[:, 8 + n:9 + n], 0), axis=0, keepdims=True)
        metav[1, n:n + 1] = row_n
        if n % HOPS == 1:
            row_n = jnp.sum(jnp.where(goes, pages, 0), axis=0, keepdims=True)
        metav[3, n:n + 1] = row_n
    to_smem2 = pltpu.make_async_copy(metav, meta, smem_sem.at[1])
    to_smem2.start()
    to_smem2.wait()

    def find():
        @pl.loop(0, 2 * NY)
        def _(k):
            column = (((y + k // 2) % NY) * NZ + z) * NX
            for p in range(CTX_PAGES):
                e = jnp.maximum(tabs[k % 2, p % 8, column + p // 8] - 1, 0)
                for variant in range(2):
                    plist[variant * 2 * NY + k, p] = meta[2 * variant, e // PLANE, e % PLANE]

    def deliver(r, k):
        return remote(ybuf.at[r, k], recv.at[r, k], ys.at[r, k], yr.at[r, k], device(k // 2, 0, k % 2))

    def near_first(j):
        return 1 + 2 * j - 3 * (j // 2)

    def hand_out(r):
        def gather(s, t):
            some = step_of(width(r, t), 16)

            @pl.loop(0, width(r, t) // some)
            def _(j):
                join[pl.ds(base_of(s, t) + j * some, some)] = arrive[r][s][t - 1][pl.ds(j * some, some)]

        @pl.loop(0, PLANE // 8)
        def _(j):
            join[pl.ds(j * 8, 8)] = home[r][pl.ds(j * 8, 8)]

        for t in range(1, HOPS + 1):
            for s in range(2):
                if t == HOPS:
                    hop(r, s, HOPS).wait_recv()
                gather(s, t)

        lists = 2 * NY if r < OPEN else 0

        def pick(k):
            for p in range(CTX_PAGES):
                ybuf[r, k, p] = join[plist[lists + k, p]]
            deliver(r, k).start()

        @pl.loop(0, NY - 1)
        def _(j):
            pick(2 * near_first(j))

        pick(1)

        @pl.loop(0, NY - 1)
        def _(j):
            pick(2 * near_first(j) + 1)

        for p in range(CTX_PAGES):
            recv[r, 0, p] = join[plist[lists, p]]

    start = start_ref[0]
    keys = CTX_PAGES * ROWS
    at = lax.broadcasted_iota(i32, (1, keys), 1)

    def attend(r, dc, h):
        tb = 2 * r + (core + dc) % 2
        allowed = at // ROWS * PAGE + at % ROWS + tb * ROWS < start
        k = recv[r, (y - 2 * h + NY) % NY * 2 + dc].reshape(keys, HEAD)
        v = recv[r, (y - 2 * h - 1 + NY) % NY * 2 + dc].reshape(keys, HEAD)

        @pl.loop(0, GROUP // PAIR, unroll=UNROLL)
        def _(g):
            n = h * GROUP + g * PAIR
            wide_row = (PAIR * PAGE, HEAD)
            q = jnp.concatenate(
                [q_ref[:, pl.ds(pl.multiple_of((n + e) * HEAD, HEAD), HEAD)] for e in range(PAIR)], axis=0
            )
            s = jnp.where(allowed, scores(q, k), -jnp.inf)
            parts = [s[:, j * HEAD:(j + 1) * HEAD] for j in range(keys // HEAD)]
            m_old = m_ref[pl.ds(n, PAIR)].reshape(wide_row)
            m = jnp.maximum(m_old, jnp.max(functools.reduce(jnp.maximum, parts), axis=1, keepdims=True))
            alpha = jnp.exp2(m_old - m)
            ps_ = [jnp.exp2(part - m) for part in parts]
            m_ref[pl.ds(n, PAIR)] = m.reshape(PAIR, PAGE, HEAD)
            l = l_ref[pl.ds(n, PAIR)].reshape(wide_row) * alpha + functools.reduce(jnp.add, ps_)
            l_ref[pl.ds(n, PAIR)] = l.reshape(PAIR, PAGE, HEAD)
            p = jnp.concatenate([part.astype(jnp.bfloat16) for part in ps_], axis=1)
            acc = acc_ref[pl.ds(n, PAIR)].reshape(wide_row) * alpha
            acc = acc + jnp.dot(p, v, preferred_element_type=jnp.float32)
            acc_ref[pl.ds(n, PAIR)] = acc.reshape(PAIR, PAGE, HEAD)

    def units(r, first, last):
        for dc in range(2):
            if first <= 2 * dc < last:

                @pl.loop(1 - dc, NY)
                def _(dy):
                    deliver(r, 2 * dy + dc).wait_recv()

            lo, hi = max(first, 2 * dc), min(last, 2 * dc + 2)
            if lo < hi:

                @pl.loop(lo - 2 * dc, hi - 2 * dc)
                def _(h):
                    attend(r, dc, h)

    if OPEN == 1:
        ring(1, 1)
    for r in range(2, ROUNDS):
        loaded(r)
        spread_all(r)
    ring(0, 2)
    ring(2, 1)
    find()
    ring(0, 3)
    ring(1, 2)
    ring(3, 1)
    ring(0, 4)
    ring(1, 3)
    ring(2, 2)
    hand_out(0)
    ring(1, 4)
    ring(2, 3)
    units(0, 0, 2)
    hand_out(1)
    ring(3, 2)
    units(0, 2, 4)
    ring(2, 4)
    units(1, 0, 1)
    ring(3, 3)
    units(1, 1, 2)
    hand_out(2)
    ring(3, 4)
    units(1, 2, 4)
    hand_out(3)
    units(2, 0, 4)
    for r in range(ROUNDS):

        @pl.loop(1, 2 * NY)
        def _(k):
            spread(r, k).wait_send()
            if r < ROUNDS - 1:
                deliver(r, k).wait_send()

        for s in range(2):
            for t in range(1, HOPS + 1):
                if r == 0 and t == 1:

                    @pl.loop(0, 2 * NY)
                    def _(k):
                        piece(s, k).wait_send()

                else:
                    hop(r, s, t).wait_send()

    pair_dy = (y % 2) + 3 * (1 - y % 2)
    for dc in range(2):
        if dc:
            deliver(3, 1).wait_recv()
        deliver(3, 2 * pair_dy + dc).wait_recv()
        attend(3, dc, y // 2)
        deliver(3, 2 * (4 - pair_dy) + dc).wait_recv()
        deliver(3, 4 + dc).wait_recv()
        attend(3, dc, 1 - y // 2)

    for n in range(KV_HEADS * GROUP):
        total = jnp.sum(l_ref[n], axis=1, keepdims=True)
        out_ref[:, n * HEAD:(n + 1) * HEAD] = (acc_ref[n] * (1.0 / total)).astype(jnp.bfloat16)

    @pl.loop(1, 2 * NY)
    def _(k):
        deliver(ROUNDS - 1, k).wait_send()


def narrow(queries, new_keys, fresh_values, lent_page_pool, page_lender, page_slot, starts):
    vmem, smem, hbm = (pl.BlockSpec(memory_space=space) for space in (pltpu.VMEM, pltpu.SMEM, pl.ANY))
    dma = pltpu.SemaphoreType.DMA
    heads = KV_HEADS * GROUP
    bf16, f32, i32 = jnp.bfloat16, jnp.float32, jnp.int32
    tiles = lambda *n: pltpu.VMEM((*n, ROWS, HEAD), bf16)
    ints = lambda *n: pltpu.VMEM((*n, 8, 128), i32)
    return pl.pallas_call(
        narrow_kernel,
        out_shape=(jax.ShapeDtypeStruct(queries.shape, bf16), jax.ShapeDtypeStruct((1, 1), i32)),
        in_specs=[smem, smem, smem, hbm, hbm, hbm, hbm],
        out_specs=(vmem, smem),
        scratch_shapes=[
            pltpu.VMEM(queries.shape, bf16), pltpu.VMEM(new_keys.shape, bf16), pltpu.VMEM(fresh_values.shape, bf16),
            [tiles(NY, 2, SLOTS) for _ in range(ROUNDS)],
            [tiles(PLANE) for _ in range(ROUNDS)],
            [[[tiles(width(r, t + 1)) for t in range(HOPS)] for _ in range(2)] for r in range(ROUNDS)],
            tiles(ROUNDS, 2, TOTAL), tiles(JOINED),
            tiles(ROUNDS, 2 * NY, CTX_PAGES), tiles(ROUNDS, 2 * NY, CTX_PAGES),
            ints(NX), ints(NZ), ints(2 * NY), ints(2), pltpu.SMEM((2, 8, 128), i32),
            ints(NZ), ints(2 * HOPS), ints(2 * HOPS), ints(2 * HOPS), pltpu.VMEM((128, 128), i32),
            ints(4), pltpu.SMEM((4, 8, 128), i32), pltpu.SMEM((16, 128), i32),
            pltpu.VMEM((heads, PAGE, HEAD), f32), pltpu.VMEM((heads, PAGE, HEAD), f32), pltpu.VMEM((heads, PAGE, HEAD), f32),
            dma((3,)), dma((ROUNDS,)), dma((ROUNDS,)), dma((2,)), dma((2, 2 * NY)), dma((2, 2 * NY)),
            dma((NX,)), dma((NX,)), dma((NZ,)), dma((NZ,)), dma((2 * NY,)), dma((2 * NY,)),
            dma((ROUNDS, 2 * NY)), dma((ROUNDS, 2 * NY)),
            dma((ROUNDS, 2, HOPS)), dma((ROUNDS, 2, HOPS)),
            dma((ROUNDS, 2 * NY)), dma((ROUNDS, 2 * NY)),
        ],
        compiler_params=pltpu.CompilerParams(
            collective_id=1, has_side_effects=True, vmem_limit_bytes=56 * 1024 * 1024
        ),
        cost_estimate=pl.CostEstimate(
            flops=4 * heads * PAGE * HEAD * (CTX_PAGES + 1) * PAGE,
            bytes_accessed=4 << 20,
            transcendentals=heads * PAGE * (CTX_PAGES + 1) * PAGE,
        ),
    )(starts, page_lender, page_slot, queries, new_keys, fresh_values, lent_page_pool)


def wide(queries, new_keys, fresh_values, lent_page_pool, page_lender, page_slot, starts):
    pages = page_lender * SLOTS + page_slot[:, None]
    table = jnp.broadcast_to(pages, (8, 128))
    vmem = pl.BlockSpec(memory_space=pltpu.VMEM)
    dma = pltpu.SemaphoreType.DMA
    heads = KV_HEADS * GROUP
    bf16, f32, i32 = jnp.bfloat16, jnp.float32, jnp.int32
    return pl.pallas_call(
        wide_kernel,
        out_shape=jax.ShapeDtypeStruct(queries.shape, bf16),
        in_specs=[
            pl.BlockSpec(memory_space=pltpu.SMEM), vmem, vmem, vmem, pl.BlockSpec(memory_space=pl.ANY), vmem,
        ],
        out_specs=vmem,
        scratch_shapes=[
            pltpu.VMEM((CHIPS, SLOTS, ROWS, HEAD), bf16),
            pltpu.VMEM((CHIPS * 2 * SLOTS, ROWS, HEAD), bf16),
            pltpu.VMEM((CHIPS, CTX_PAGES, ROWS, HEAD), bf16),
            pltpu.VMEM((CHIPS, CTX_PAGES, ROWS, HEAD), bf16),
            pltpu.VMEM((NX, 8, 128), i32),
            pltpu.VMEM((CHIPS, 8, 128), i32),
            pltpu.VMEM((8, 128), i32),
            pltpu.SMEM((8, 128), i32),
            pltpu.VMEM((heads, PAGE, HEAD), f32),
            pltpu.VMEM((heads, PAGE, HEAD), f32),
            pltpu.VMEM((heads, PAGE, HEAD), f32),
            dma, dma, dma,
            dma((NX,)), dma((NX,)),
            dma((CHIPS,)), dma((CHIPS,)),
            dma((CHIPS,)), dma((CHIPS,)),
            dma((CHIPS,)), dma((CHIPS,)),
            dma((CHIPS,)), dma((CHIPS,)),
        ],
        compiler_params=pltpu.CompilerParams(
            collective_id=0, has_side_effects=True, vmem_limit_bytes=48 * 1024 * 1024
        ),
        cost_estimate=pl.CostEstimate(
            flops=4 * heads * PAGE * HEAD * (CTX_PAGES + 1) * PAGE,
            bytes_accessed=4 << 20,
            transcendentals=heads * PAGE * (CTX_PAGES + 1) * PAGE,
        ),
    )(starts, queries, new_keys, fresh_values, lent_page_pool, table)


def local(*args):
    out, over = narrow(*args)
    return lax.cond(over[0, 0] > 0, lambda: wide(*args), lambda: out)


def solution(mesh):
    in_specs = (
        P("inst", "tp"),
        P("inst", "tp"),
        P("inst", "tp"),
        P("inst", None, None, "tp"),
        P(("inst", "tp"), None),
        P(("inst", "tp")),
        P("inst"),
    )
    return jax.shard_map(local, mesh=mesh, in_specs=in_specs, out_specs=P("inst", "tp"), check_vma=False)
```
